512 devices in a mesh: coil: 8 (over y), pencil: 32 (over z, x_lo, core), frame: 2 (over x_hi).
Axes of the slice: x: 4 (x_hi: 2, x_lo: 2; x = x_hi * 2 + x_lo), y: 8, z: 8, core: 2. Of those that a mesh axis runs over, the one named last changes fastest.
Arguments:
- kdata: bfloat16 [2, 8, 2, 96, 256, 256], P('frame', 'coil', None, None, 'pencil'), may hold values from -6 to 6
- sampling: int32 [2, 96, 256], P('frame'), may hold values 0 or 1
- sensitivity: bfloat16 [8, 2, 96, 256, 256], P('coil', None, 'pencil'), may hold values from -3 to 3
- baseline: bfloat16 [2, 96, 256, 256], P(None, 'pencil', ('coil', 'frame')), may hold values from -6 to 6
- ktrans: bfloat16 [96, 256, 256], P('pencil', ('coil', 'frame')), may hold values from 0 to 0.59765625
- plasma_volume: bfloat16 [96, 256, 256], P('pencil', ('coil', 'frame')), may hold values from 0 to 0.29882812
- arterial: float32 [2], P('frame'), may hold values from 0.5 to 4
- arterial_integral: float32 [2], P('frame'), may hold values from 0.5 to 4
Outputs:
- grad_ktrans: float32 [96, 256, 256], P('pencil', ('coil', 'frame'))
- grad_volume: float32 [96, 256, 256], P('pencil', ('coil', 'frame'))
The draws below stay inside these ranges and needn't reach their ends.
All inputs are finite; a program needn't handle non-finite values. No bound on the sum of `sampling` on one device may be relied on, other than what follows from the above.
Results may differ from the reference program's by a relative error of at most 0.0023.
Values may be sent and summed in bfloat16 or wider, within the bound.
A program may use at most 64 MiB of HBM per device.

```python
import math
import jax
import jax.numpy as jnp
from jax import lax

NX = 256
NY = 256
NZ = 96
COILS = 8
FRAMES = 2


def set_ends(values, key, smallest, high):
    spot = [jax.random.randint(jax.random.fold_in(key, axis), (), 0, length) for axis, length in enumerate(values.shape)]
    widest = values.shape.index(max(values.shape))
    neighbour = spot[:widest] + [(spot[widest] + 1) % values.shape[widest]] + spot[widest + 1:]
    return values.at[tuple(spot)].set(smallest).at[tuple(neighbour)].set(high)


def level_of(key, dims, shards, least, largest):
    def one(dim, parts):
        heights = jax.random.uniform(jax.random.fold_in(jax.random.fold_in(key, 6), dim), (parts,), jnp.float32, least / len(shards), largest / len(shards))
        return jnp.repeat(jnp.exp(heights), dims[dim] // parts).reshape((-1,) + (1,) * (len(dims) - dim - 1))

    factor_of = one(*shards[0])
    for cut in shards[1:]:
        factor_of = factor_of * one(*cut)
    return factor_of


def bell_draw(own_key, shape, width, reach, pieces=(), held_as=jnp.bfloat16):
    array = jax.random.normal(own_key, shape, jnp.float32) * width
    if len(pieces) > 0:
        array = level_of(own_key, shape, pieces, -0.22, 0.18) * array
    return jnp.clip(array, min=-reach, max=reach).astype(held_as)


def setup_inputs(seed: int = 0) -> dict:
    streams_of = jax.random.split(jax.random.key(seed), 9)
    return {
        "kdata": bell_draw(streams_of[0], (FRAMES, COILS, 2, NZ, NX, NY), 1.0, 6.0, ((0, 2), (1, 8), (4, 32))),
        "sampling": set_ends((jax.random.randint(streams_of[1], (FRAMES, NZ, NY), 0, 3) < 1).astype(jnp.int32), jax.random.fold_in(streams_of[1], 1), 0, 1),
        "sensitivity": bell_draw(streams_of[2], (COILS, 2, NZ, NX, NY), 0.5, 3.0, ((0, 8), (2, 32))),
        "baseline": bell_draw(streams_of[3], (2, NZ, NX, NY), 1.0, 6.0, ((1, 32), (2, 16))),
        "ktrans": jnp.clip(0.59765625 * jax.random.uniform(streams_of[4], (NZ, NX, NY), jnp.float32) ** level_of(streams_of[4], (NZ, NX, NY), ((0, 32), (1, 16)), -0.2, 0.2), 0.0, 0.59765625).astype(jnp.bfloat16),
        "plasma_volume": jnp.clip(0.29882812 * jax.random.uniform(streams_of[5], (NZ, NX, NY), jnp.float32) ** level_of(streams_of[5], (NZ, NX, NY), ((0, 32), (1, 16)), -0.2, 0.2), 0.0, 0.29882812).astype(jnp.bfloat16),
        "arterial": jnp.clip(jnp.exp(math.log(4.0) - 2.0794415 * jax.random.uniform(streams_of[6], (FRAMES,), jnp.float32) ** level_of(streams_of[6], (FRAMES,), ((0, 2),), -0.2, 0.2)), 0.5, 4.0),
        "arterial_integral": jnp.clip(jnp.exp(math.log(4.0) - 2.0794415 * jax.random.uniform(streams_of[7], (FRAMES,), jnp.float32) ** level_of(streams_of[7], (FRAMES,), ((0, 2),), -0.2, 0.2)), 0.5, 4.0),
    }


def tables(size):
    index = jnp.arange(size, dtype=jnp.int32)
    product = index[:, None] * index[None, :] % size
    angle = product.astype(jnp.float32) * (2.0 * math.pi / size)
    scale = 1.0 / math.sqrt(size)
    return ((jnp.cos(angle) * scale).astype(jnp.bfloat16), (jnp.sin(angle) * scale).astype(jnp.bfloat16))

def transform(pair, form, cos_t, sin_t, sign, out_type):
    real = pair[0].astype(jnp.float32)
    imag = pair[1].astype(jnp.float32)
    cosf = cos_t.astype(jnp.float32)
    sinf = sin_t.astype(jnp.float32)
    high = lax.Precision.HIGHEST
    real_cos = jnp.einsum(form, real, cosf, precision=high)
    real_sin = jnp.einsum(form, real, sinf, precision=high)
    imag_cos = jnp.einsum(form, imag, cosf, precision=high)
    imag_sin = jnp.einsum(form, imag, sinf, precision=high)
    return jnp.stack([real_cos + sign * imag_sin, imag_cos - sign * real_sin]).astype(out_type)

def reference(kdata, sampling, sensitivity, baseline, ktrans, plasma_volume, arterial, arterial_integral):
    cos_x, sin_x = tables(NX)
    cos_y, sin_y = tables(NY)
    cos_z, sin_z = tables(NZ)
    base_re = baseline[0].astype(jnp.float32)
    base_im = baseline[1].astype(jnp.float32)
    grad_k = jnp.zeros((NZ, NX, NY), jnp.float32)
    grad_v = jnp.zeros((NZ, NX, NY), jnp.float32)
    for frame in range(FRAMES):
        factor = 1.0 + arterial_integral[frame] * ktrans.astype(jnp.float32) + arterial[frame] * plasma_volume.astype(jnp.float32)
        frame_re = base_re * factor
        frame_im = base_im * factor
        keep = sampling[frame].astype(jnp.float32)[:, None, :]

        def per_coil(carry, items):
            sens, measured = items
            sens_re = sens[0].astype(jnp.float32)
            sens_im = sens[1].astype(jnp.float32)
            coil = jnp.stack([sens_re * frame_re - sens_im * frame_im, sens_re * frame_im + sens_im * frame_re])
            after_y = transform(coil, 'zxy,yk->zxk', cos_y, sin_y, 1.0, jnp.float32)
            after_xy = transform(after_y, 'zxy,xk->zky', cos_x, sin_x, 1.0, jnp.bfloat16)
            kspace = transform(after_xy, 'zxy,zk->kxy', cos_z, sin_z, 1.0, jnp.float32)
            resid = keep[None] * (kspace - measured.astype(jnp.float32))
            back_z = transform(resid, 'zxy,zk->kxy', cos_z, sin_z, -1.0, jnp.bfloat16)
            back_zx = transform(back_z, 'zxy,xk->zky', cos_x, sin_x, -1.0, jnp.float32)
            back = transform(back_zx, 'zxy,yk->zxk', cos_y, sin_y, -1.0, jnp.float32)
            adj_re = sens_re * back[0] + sens_im * back[1]
            adj_im = sens_re * back[1] - sens_im * back[0]
            return ((carry[0] + adj_re, carry[1] + adj_im), None)
        start = (jnp.zeros((NZ, NX, NY), jnp.float32), jnp.zeros((NZ, NX, NY), jnp.float32))
        total, unused = lax.scan(per_coil, start, (sensitivity, kdata[frame]))
        projection = base_re * total[0] + base_im * total[1]
        grad_k = grad_k + arterial_integral[frame] * projection
        grad_v = grad_v + arterial[frame] * projection
    return (grad_k, grad_v)
```

```python
import math

import jax
import jax.numpy as jnp
import numpy as np
from jax import lax
from jax.experimental import pallas as pl
from jax.experimental.pallas import tpu as pltpu
from jax.sharding import PartitionSpec as P

MESH = pl.DeviceIdType.MESH
F32 = jnp.float32
BF16 = jnp.bfloat16


def tables(size):
    index = np.arange(size)
    product = index[:, None] * index[None, :] % size
    angle = product.astype(np.float32) * np.float32(2.0 * math.pi / size)
    scale = np.float32(1.0 / math.sqrt(size))
    return (
        (np.cos(angle.astype(np.float64)).astype(np.float32) * scale).astype(BF16),
        (np.sin(angle.astype(np.float64)).astype(np.float32) * scale).astype(BF16),
    )


def complex_table(size):
    cos_t, sin_t = tables(size)
    return np.stack(
        [
            np.stack([cos_t.T, sin_t.T], axis=1),
            np.stack([-sin_t.T, cos_t.T], axis=1),
        ]
    )


def all_tables(nx, ny, nz, pencils):
    lines, planes = nx // pencils, nz // pencils
    cos_y, sin_y = tables(ny)
    rows_y = np.concatenate([cos_y, sin_y], axis=1)
    full_x = complex_table(nx)
    forward_x = (
        full_x.reshape(2, pencils, lines, 2 * nx)
        .transpose(1, 0, 2, 3)
        .reshape(2 * nx, 2 * nx)
    )
    inverse_x = np.ascontiguousarray(forward_x.T)
    full_z = complex_table(nz)
    spread = np.einsum(
        "akbz,ij->akibzj", full_z.astype(np.float32), np.eye(lines, dtype=np.float32)
    )
    spread = spread.reshape(2, nz, lines, 2, pencils, planes, lines)
    forward_z = (
        spread.transpose(5, 0, 1, 2, 4, 3, 6)
        .reshape(planes, 2 * nz * lines, pencils * 2 * lines)
        .astype(BF16)
    )
    inverse_z = np.ascontiguousarray(forward_z.transpose(0, 2, 1))
    return rows_y, forward_x, inverse_x, forward_z, inverse_z


def dot(a, b):
    return jnp.dot(a, b, preferred_element_type=F32)


def split(value):
    high = value.astype(BF16)
    return high, (value - high.astype(F32)).astype(BF16)


def kernel(
    sizes,
    base_in,
    ktrans_in,
    volume_in,
    arterial,
    integral,
    sens_in,
    kdata_in,
    sampling_in,
    rows_y_in,
    forward_x_in,
    inverse_x_in,
    forward_z_in,
    inverse_z_in,
    out_k,
    out_v,
    maps,
    sens,
    kdata,
    sampling,
    rows_y,
    forward_x,
    inverse_x,
    forward_z,
    inverse_z,
    field,
    send_f,
    recv_f,
    kspace,
    res_high,
    res_low,
    send_b,
    recv_b,
    send_p,
    recv_p,
    weights,
    own_sem,
    load_sem,
    maps_send,
    maps_recv,
    fsend_sem,
    frecv_sem,
    bsend_sem,
    brecv_sem,
    psend_sem,
    precv_sem,
    wsend_sem,
    wrecv_sem,
):
    coils, pencils, frames = sizes
    planes = maps.shape[0]
    nx = field.shape[2]
    c = lax.axis_index("coil")
    p = lax.axis_index("pencil")
    t = lax.axis_index("frame")
    me = c * frames + t
    other = 1 - t
    right = lax.rem(c + 1, coils)
    left = lax.rem(c + coils - 1, coils)

    own = [
        pltpu.make_async_copy(base_in.at[0], maps.at[:, 0, me], own_sem.at[0]),
        pltpu.make_async_copy(base_in.at[1], maps.at[:, 1, me], own_sem.at[1]),
        pltpu.make_async_copy(ktrans_in, maps.at[:, 2, me], own_sem.at[2]),
        pltpu.make_async_copy(volume_in, maps.at[:, 3, me], own_sem.at[3]),
    ]
    for copy in own:
        copy.start()
    pairs = [
        (rows_y_in, rows_y),
        (sens_in, sens),
        (forward_x_in, forward_x),
        (forward_z_in, forward_z),
        (kdata_in, kdata),
        (sampling_in, sampling),
        (inverse_z_in, inverse_z),
        (inverse_x_in, inverse_x),
    ]
    loads = [
        pltpu.make_async_copy(src, dst, load_sem.at[n])
        for n, (src, dst) in enumerate(pairs)
    ]
    for copy in loads:
        copy.start()

    barrier = pltpu.get_barrier_semaphore()

    def greet_pencil(d, carry):
        peer = lax.rem(p + d, pencils)
        pl.semaphore_signal(barrier, inc=1, device_id={"pencil": peer}, device_id_type=MESH)
        return carry

    lax.fori_loop(1, pencils, greet_pencil, 0)

    def greet_maps(d, carry):
        peer = lax.rem(me + d, coils * frames)
        pl.semaphore_signal(
            barrier,
            inc=1,
            device_id={"coil": peer // frames, "frame": lax.rem(peer, frames)},
            device_id_type=MESH,
        )
        return carry

    lax.fori_loop(1, coils * frames, greet_maps, 0)
    pl.semaphore_wait(barrier, pencils - 1 + coils * frames - 1)

    weights[t, 0] = jnp.full(weights.shape[2:], integral[0], F32)
    weights[t, 1] = jnp.full(weights.shape[2:], arterial[0], F32)
    weight_copy = pltpu.make_async_remote_copy(
        weights.at[t],
        weights.at[t],
        wsend_sem,
        wrecv_sem,
        device_id={"frame": other},
        device_id_type=MESH,
    )
    weight_copy.start()

    def push(i, owner, axis, to):
        pltpu.make_async_remote_copy(
            maps.at[i, :, owner],
            maps.at[i, :, owner],
            maps_send.at[i],
            maps_recv.at[i, owner],
            device_id={axis: to},
            device_id_type=MESH,
        ).start()

    def arrive(i, owner):
        block = maps.at[i, :, owner]
        pltpu.make_async_copy(block, block, maps_recv.at[i, owner]).wait()

    def owner_at(shift, frame):
        return lax.rem(c + shift + coils, coils) * frames + frame

    def gather_start(i):
        push(i, me, "frame", other)
        push(i, me, "coil", right)
        push(i, me, "coil", left)

    def gather_cross(i):
        mine = owner_at(0, other)
        arrive(i, mine)
        push(i, mine, "coil", left)
        push(i, mine, "coil", right)

    half = coils // 2

    def gather_step(i, s):
        for frame, far_right in ((t, True), (other, False)):
            if s < half or far_right:
                owner = owner_at(-s, frame)
                arrive(i, owner)
                if s < (half if far_right else half - 1):
                    push(i, owner, "coil", right)
            if s < half or not far_right:
                owner = owner_at(s, frame)
                arrive(i, owner)
                if s < (half - 1 if far_right else half):
                    push(i, owner, "coil", left)

    def forward(i):
        shape = (nx, maps.shape[-1])
        base_re = maps[i, 0].reshape(shape).astype(F32)
        base_im = maps[i, 1].reshape(shape).astype(F32)
        factor = (
            1.0
            + integral[0] * maps[i, 2].reshape(shape).astype(F32)
            + arterial[0] * maps[i, 3].reshape(shape).astype(F32)
        )
        sens_re = sens[0, i].astype(F32)
        sens_im = sens[1, i].astype(F32)
        field_re = sens_re * base_re - sens_im * base_im
        field_im = sens_re * base_im + sens_im * base_re
        field[i, 0] = field_re
        field[i, 1] = field_im
        high, low = split(jnp.concatenate([field_re * factor, field_im * factor], axis=0))
        y = dot(high, rows_y[...]) + dot(low, rows_y[...])
        ny = shape[1]
        high, low = split(
            jnp.concatenate(
                [y[:nx, :ny] + y[nx:, ny:], y[nx:, :ny] - y[:nx, ny:]], axis=0
            )
        )
        x = dot(forward_x[...], high) + dot(forward_x[...], low)
        send_f[i] = x.astype(BF16).reshape(send_f.shape[1:])
        recv_f[i, p] = send_f[i, p]
        exchange(send_f, recv_f, fsend_sem, frecv_sem, i)

    def exchange(src, dst, send_sem, recv_sem, i):
        def one(d, carry):
            peer = lax.rem(p + d, pencils)
            pltpu.make_async_remote_copy(
                src.at[i, peer],
                dst.at[i, p],
                send_sem.at[i],
                recv_sem.at[i],
                device_id={"pencil": peer},
                device_id_type=MESH,
            ).start()
            return carry

        lax.fori_loop(1, pencils, one, 0)

    def wait_bytes(ref, i, count, sem):
        view = ref.at[i, pl.ds(0, count)]
        pltpu.make_async_copy(view, view, sem.at[i]).wait()

    for copy in own:
        copy.wait()
    for i in range(planes):
        gather_start(i)
    for i in range(planes):
        gather_cross(i)
    for s in range(1, half + 1):
        gather_step(0, s)
    for copy in loads[:3]:
        copy.wait()
    forward(0)
    for i in range(1, planes):
        for s in range(1, half + 1):
            gather_step(i, s)
        forward(i)

    loads[3].wait()
    block = nx
    blocks = kspace.shape[0] // block
    for i in range(planes):
        wait_bytes(recv_f, i, pencils - 1, frecv_sem)
        lines = recv_f[i].reshape(-1, recv_f.shape[-1])

        def add(r, carry):
            rows = pl.ds(pl.multiple_of(r * block, block), block)
            term = dot(forward_z[i, rows, :], lines)
            if i > 0:
                term = term + kspace[rows, :]
            kspace[rows, :] = term
            return carry

        lax.fori_loop(0, blocks, add, 0)
    for copy in loads[4:7]:
        copy.wait()
    some = block // kdata.shape[2]

    def residual(r, carry):
        rows = pl.ds(pl.multiple_of(r * block, block), block)
        part, first = r // (blocks // 2), lax.rem(r, blocks // 2) * some
        first = pl.multiple_of(first, some)
        measured = kdata[part, pl.ds(first, some)].astype(F32)
        keep = sampling[pl.ds(first, some), :].astype(F32)[:, None, :]
        value = keep * (kspace[rows, :].reshape(measured.shape) - measured)
        high, low = split(value.reshape(block, -1))
        res_high[rows, :] = high
        res_low[rows, :] = low
        return carry

    lax.fori_loop(0, blocks, residual, 0)
    for i in range(planes):
        x = dot(inverse_z[i], res_high[...]) + dot(inverse_z[i], res_low[...])
        send_b[i] = x.astype(BF16).reshape(send_b.shape[1:])
        recv_b[i, p] = send_b[i, p]
        exchange(send_b, recv_b, bsend_sem, brecv_sem, i)

    loads[7].wait()
    owners = coils * frames
    for i in range(planes):
        wait_bytes(recv_b, i, pencils - 1, brecv_sem)
        x = dot(inverse_x[...], recv_b[i].reshape(-1, recv_b.shape[-1]))
        high, low = split(x)
        y = dot(high, rows_y[...]) + dot(low, rows_y[...])
        ny = recv_b.shape[-1]
        back_re = y[:nx, :ny] - y[nx:, ny:]
        back_im = y[nx:, :ny] + y[:nx, ny:]
        terms = field[i, 0] * back_re + field[i, 1] * back_im
        send_p[i] = terms.astype(BF16).reshape(send_p.shape[1:])
        recv_p[i, me] = send_p[i, me]

        def hand(d, carry):
            peer = lax.rem(me + d, owners)
            pltpu.make_async_remote_copy(
                send_p.at[i, peer],
                recv_p.at[i, me],
                psend_sem.at[i],
                precv_sem.at[i],
                device_id={"coil": peer // frames, "frame": lax.rem(peer, frames)},
                device_id_type=MESH,
            ).start()
            return carry

        lax.fori_loop(1, owners, hand, 0)

    weight_copy.wait()
    for i in range(planes):
        wait_bytes(recv_p, i, owners - 1, precv_sem)
        totals = [
            sum(recv_p[i, n * frames + f].astype(F32) for n in range(coils))
            for f in range(frames)
        ]
        out_k[i] = sum(weights[f, 0] * totals[f] for f in range(frames))
        out_v[i] = sum(weights[f, 1] * totals[f] for f in range(frames))

    for i in range(planes):
        view = maps.at[i, :, pl.ds(0, owners - 1)]
        pltpu.make_async_copy(view, view, maps_send.at[i]).wait()
        wait_bytes(send_f, i, pencils - 1, fsend_sem)
        wait_bytes(send_b, i, pencils - 1, bsend_sem)
        wait_bytes(send_p, i, owners - 1, psend_sem)


def solution(mesh):
    coils, pencils, frames = mesh.shape["coil"], mesh.shape["pencil"], mesh.shape["frame"]

    def per_device(
        kdata, sampling, sensitivity, baseline, ktrans, plasma_volume, arterial, arterial_integral
    ):
        planes, rows, ny = ktrans.shape
        nx = sensitivity.shape[3]
        nz = kdata.shape[3]
        lines = kdata.shape[4]
        owners = coils * frames
        tabs = all_tables(nx, ny, nz, pencils)
        hbm = pl.BlockSpec(memory_space=pl.ANY)
        smem = pl.BlockSpec(memory_space=pltpu.SMEM)
        vmem = pl.BlockSpec(memory_space=pltpu.VMEM)
        out = jax.ShapeDtypeStruct((planes, rows, ny), F32)
        dma = pltpu.SemaphoreType.DMA
        blocks = (planes, pencils, 2 * lines, ny)
        return pl.pallas_call(
            lambda *refs: kernel((coils, pencils, frames), *refs),
            out_shape=(out, out),
            in_specs=[hbm, hbm, hbm, smem, smem] + [hbm] * 8,
            out_specs=(vmem, vmem),
            scratch_shapes=[
                pltpu.VMEM((planes, 4, owners, rows, ny), BF16),
                pltpu.VMEM((2, planes, nx, ny), BF16),
                pltpu.VMEM((2, nz, lines, ny), BF16),
                pltpu.VMEM((nz, ny), jnp.int32),
                *[pltpu.VMEM(tab.shape, BF16) for tab in tabs],
                pltpu.VMEM((planes, 2, nx, ny), F32),
                pltpu.VMEM(blocks, BF16),
                pltpu.VMEM(blocks, BF16),
                pltpu.VMEM((2 * nz * lines, ny), F32),
                pltpu.VMEM((2 * nz * lines, ny), BF16),
                pltpu.VMEM((2 * nz * lines, ny), BF16),
                pltpu.VMEM(blocks, BF16),
                pltpu.VMEM(blocks, BF16),
                pltpu.VMEM((planes, owners, rows, ny), BF16),
                pltpu.VMEM((planes, owners, rows, ny), BF16),
                pltpu.VMEM((frames, 2, rows, ny), F32),
                dma((4,)),
                dma((8,)),
                dma((planes,)),
                dma((planes, owners)),
                dma((planes,)),
                dma((planes,)),
                dma((planes,)),
                dma((planes,)),
                dma((planes,)),
                dma((planes,)),
                dma,
                dma,
            ],
            compiler_params=pltpu.CompilerParams(
                collective_id=0, has_side_effects=True, vmem_limit_bytes=48 * 1024 * 1024
            ),
        )(
            baseline,
            ktrans,
            plasma_volume,
            arterial,
            arterial_integral,
            sensitivity[0],
            kdata[0, 0],
            sampling[0],
            *[jnp.asarray(tab) for tab in tabs],
        )

    in_specs = (
        P("frame", "coil", None, None, "pencil", None),
        P("frame", None, None),
        P("coil", None, "pencil", None, None),
        P(None, "pencil", ("coil", "frame"), None),
        P("pencil", ("coil", "frame"), None),
        P("pencil", ("coil", "frame"), None),
        P("frame"),
        P("frame"),
    )
    out_specs = (P("pencil", ("coil", "frame"), None), P("pencil", ("coil", "frame"), None))
    return jax.shard_map(
        per_device, mesh=mesh, in_specs=in_specs, out_specs=out_specs, check_vma=False
    )
```

```python
import math

import jax
import jax.numpy as jnp
import numpy as np
from jax import lax
from jax.experimental import pallas as pl
from jax.experimental.pallas import tpu as pltpu
from jax.sharding import PartitionSpec as P

MESH = pl.DeviceIdType.MESH
F32 = jnp.float32
BF16 = jnp.bfloat16


def tables(size):
    index = np.arange(size)
    product = index[:, None] * index[None, :] % size
    angle = product.astype(np.float32) * np.float32(2.0 * math.pi / size)
    scale = np.float32(1.0 / math.sqrt(size))
    return (
        (np.cos(angle.astype(np.float64)).astype(np.float32) * scale).astype(BF16),
        (np.sin(angle.astype(np.float64)).astype(np.float32) * scale).astype(BF16),
    )


def complex_table(size):
    cos_t, sin_t = tables(size)
    return np.stack(
        [
            np.stack([cos_t.T, sin_t.T], axis=1),
            np.stack([-sin_t.T, cos_t.T], axis=1),
        ]
    )


def all_tables(nx, ny, nz, pencils):
    lines, planes = nx // pencils, nz // pencils
    cos_y, sin_y = tables(ny)
    rows_y = np.concatenate([cos_y, sin_y], axis=1)
    full_x = complex_table(nx)
    forward_x = (
        full_x.reshape(2, pencils, lines, 2 * nx)
        .transpose(1, 0, 2, 3)
        .reshape(2 * nx, 2 * nx)
    )
    inverse_x = np.ascontiguousarray(forward_x.T)
    full_z = complex_table(nz)
    spread = np.einsum(
        "akbz,ij->akibzj", full_z.astype(np.float32), np.eye(lines, dtype=np.float32)
    )
    spread = spread.reshape(2, nz, lines, 2, pencils, planes, lines)
    forward_z = (
        spread.transpose(5, 0, 1, 2, 4, 3, 6)
        .reshape(planes, 2 * nz * lines, pencils * 2 * lines)
        .astype(BF16)
    )
    inverse_z = np.ascontiguousarray(forward_z.transpose(0, 2, 1))
    return rows_y, forward_x, inverse_x, forward_z, inverse_z


def dot(a, b):
    return jnp.dot(a, b, preferred_element_type=F32)


def split(value):
    high = value.astype(BF16)
    return high, (value - high.astype(F32)).astype(BF16)


def kernel(
    sizes,
    base_in,
    ktrans_in,
    volume_in,
    arterial,
    integral,
    sens_in,
    kdata_in,
    sampling_in,
    rows_y_in,
    forward_x_in,
    inverse_x_in,
    forward_z_in,
    inverse_z_in,
    out_k,
    out_v,
    own_base,
    own_params,
    own_frames,
    images,
    bases,
    sens,
    kdata,
    sampling,
    rows_y,
    forward_x,
    inverse_x,
    forward_z,
    inverse_z,
    send_f,
    recv_f,
    kspace,
    res_high,
    res_low,
    send_b,
    recv_b,
    send_p,
    recv_p,
    weights,
    own_sem,
    load_sem,
    isend_sem,
    irecv_sem,
    base_send,
    base_recv,
    fsend_sem,
    frecv_sem,
    bsend_sem,
    brecv_sem,
    psend_sem,
    precv_sem,
    wsend_sem,
    wrecv_sem,
):
    coils, pencils, frames = sizes
    planes, owners = images.shape[:2]
    nx = sens.shape[2]
    c = lax.axis_index("coil")
    p = lax.axis_index("pencil")
    t = lax.axis_index("frame")
    me = c * frames + t
    other = 1 - t

    own = [
        pltpu.make_async_copy(base_in.at[0], own_base.at[:, 0], own_sem.at[0]),
        pltpu.make_async_copy(base_in.at[1], own_base.at[:, 1], own_sem.at[1]),
        pltpu.make_async_copy(ktrans_in, own_params.at[0], own_sem.at[2]),
        pltpu.make_async_copy(volume_in, own_params.at[1], own_sem.at[3]),
    ]
    for copy in own:
        copy.start()
    pairs = [
        (rows_y_in, rows_y),
        (sens_in, sens),
        (forward_x_in, forward_x),
        (forward_z_in, forward_z),
        (kdata_in, kdata),
        (sampling_in, sampling),
        (inverse_z_in, inverse_z),
        (inverse_x_in, inverse_x),
    ]
    loads = [
        pltpu.make_async_copy(src, dst, load_sem.at[n])
        for n, (src, dst) in enumerate(pairs)
    ]
    for copy in loads:
        copy.start()

    barrier = pltpu.get_barrier_semaphore()

    def greet_pencil(d, carry):
        peer = lax.rem(p + d, pencils)
        pl.semaphore_signal(barrier, inc=1, device_id={"pencil": peer}, device_id_type=MESH)
        return carry

    lax.fori_loop(1, pencils, greet_pencil, 0)

    def greet_maps(d, carry):
        peer = lax.rem(me + d, coils * frames)
        pl.semaphore_signal(
            barrier,
            inc=1,
            device_id={"coil": peer // frames, "frame": lax.rem(peer, frames)},
            device_id_type=MESH,
        )
        return carry

    lax.fori_loop(1, coils * frames, greet_maps, 0)

    weights[t, 0] = jnp.full(weights.shape[2:], integral[0], F32)
    weights[t, 1] = jnp.full(weights.shape[2:], arterial[0], F32)

    def frame_rows(frame):
        factor = (
            1.0
            + weights[frame, 0] * own_params[0].astype(F32)
            + weights[frame, 1] * own_params[1].astype(F32)
        )
        own_frames[frame] = (own_base[...].astype(F32) * factor[:, None]).astype(BF16)

    for copy in own:
        copy.wait()
    frame_rows(t)
    pl.semaphore_wait(barrier, pencils - 1 + owners - 1)
    weight_copy = pltpu.make_async_remote_copy(
        weights.at[t],
        weights.at[t],
        wsend_sem,
        wrecv_sem,
        device_id={"frame": other},
        device_id_type=MESH,
    )
    weight_copy.start()

    def images_to(i, frame, first):
        def one(d, carry):
            peer = lax.rem(c + d, coils)
            pltpu.make_async_remote_copy(
                own_frames.at[frame, i],
                images.at[i, me],
                isend_sem.at[i],
                irecv_sem.at[i],
                device_id={"coil": peer, "frame": frame},
                device_id_type=MESH,
            ).start()
            return carry

        lax.fori_loop(first, coils, one, 0)

    def bases_to(d, carry):
        peer = lax.rem(me + d, owners)
        pltpu.make_async_remote_copy(
            own_base,
            bases.at[me],
            base_send,
            base_recv,
            device_id={"coil": peer // frames, "frame": lax.rem(peer, frames)},
            device_id_type=MESH,
        ).start()
        return carry

    def forward(i):
        shape = (nx, images.shape[-1])
        frame_re = images[i, :, 0].reshape(shape).astype(F32)
        frame_im = images[i, :, 1].reshape(shape).astype(F32)
        sens_re = sens[0, i].astype(F32)
        sens_im = sens[1, i].astype(F32)
        high, low = split(
            jnp.concatenate(
                [
                    sens_re * frame_re - sens_im * frame_im,
                    sens_re * frame_im + sens_im * frame_re,
                ],
                axis=0,
            )
        )
        y = dot(high, rows_y[...]) + dot(low, rows_y[...])
        ny = shape[1]
        high, low = split(
            jnp.concatenate(
                [y[:nx, :ny] + y[nx:, ny:], y[nx:, :ny] - y[:nx, ny:]], axis=0
            )
        )
        x = dot(forward_x[...], high) + dot(forward_x[...], low)
        send_f[i] = x.astype(BF16).reshape(send_f.shape[1:])
        recv_f[i, p] = send_f[i, p]
        exchange(send_f, recv_f, fsend_sem, frecv_sem, i)

    def exchange(src, dst, send_sem, recv_sem, i):
        def one(d, carry):
            peer = lax.rem(p + d, pencils)
            pltpu.make_async_remote_copy(
                src.at[i, peer],
                dst.at[i, p],
                send_sem.at[i],
                recv_sem.at[i],
                device_id={"pencil": peer},
                device_id_type=MESH,
            ).start()
            return carry

        lax.fori_loop(1, pencils, one, 0)

    def wait_bytes(ref, i, count, sem):
        view = ref.at[i, pl.ds(0, count)]
        pltpu.make_async_copy(view, view, sem.at[i]).wait()

    images_to(0, t, 1)
    weight_copy.wait()
    frame_rows(other)
    images_to(0, other, 0)
    for i in range(1, planes):
        images_to(i, t, 1)
        images_to(i, other, 0)
    images[:, me] = own_frames[t]
    bases[me] = own_base[...]
    for copy in loads[:3]:
        copy.wait()
    for i in range(planes):
        wait_bytes(images, i, owners - 1, irecv_sem)
        forward(i)
    lax.fori_loop(1, owners, bases_to, 0)

    loads[3].wait()
    for i in range(planes):
        wait_bytes(recv_f, i, pencils - 1, frecv_sem)
        lines = recv_f[i].reshape(-1, recv_f.shape[-1])

        term = dot(forward_z[i], lines)
        if i > 0:
            term = term + kspace[...]
        kspace[...] = term
    for copy in loads[4:7]:
        copy.wait()
    block = nx
    blocks = kspace.shape[0] // block
    some = block // kdata.shape[2]

    def residual(r, carry):
        rows = pl.ds(pl.multiple_of(r * block, block), block)
        part, first = r // (blocks // 2), lax.rem(r, blocks // 2) * some
        first = pl.multiple_of(first, some)
        measured = kdata[part, pl.ds(first, some)].astype(F32)
        keep = sampling[pl.ds(first, some), :].astype(F32)[:, None, :]
        value = keep * (kspace[rows, :].reshape(measured.shape) - measured)
        high, low = split(value.reshape(block, -1))
        res_high[rows, :] = high
        res_low[rows, :] = low
        return carry

    lax.fori_loop(0, blocks, residual, 0)
    for i in range(planes):
        x = dot(inverse_z[i], res_high[...]) + dot(inverse_z[i], res_low[...])
        send_b[i] = x.astype(BF16).reshape(send_b.shape[1:])
        recv_b[i, p] = send_b[i, p]
        exchange(send_b, recv_b, bsend_sem, brecv_sem, i)

    loads[7].wait()
    base_blocks = bases.at[pl.ds(0, owners - 1)]
    pltpu.make_async_copy(base_blocks, base_blocks, base_recv).wait()
    for i in range(planes):
        wait_bytes(recv_b, i, pencils - 1, brecv_sem)
        x = dot(inverse_x[...], recv_b[i].reshape(-1, recv_b.shape[-1]))
        high, low = split(x)
        y = dot(high, rows_y[...]) + dot(low, rows_y[...])
        ny = recv_b.shape[-1]
        back_re = y[:nx, :ny] - y[nx:, ny:]
        back_im = y[nx:, :ny] + y[:nx, ny:]
        sens_re = sens[0, i].astype(F32)
        sens_im = sens[1, i].astype(F32)
        adj_re = sens_re * back_re + sens_im * back_im
        adj_im = sens_re * back_im - sens_im * back_re
        base_re = bases[:, i, 0].reshape(nx, ny).astype(F32)
        base_im = bases[:, i, 1].reshape(nx, ny).astype(F32)
        terms = base_re * adj_re + base_im * adj_im
        send_p[i] = terms.astype(BF16).reshape(send_p.shape[1:])
        recv_p[i, me] = send_p[i, me]

        def hand(d, carry):
            peer = lax.rem(me + d, owners)
            pltpu.make_async_remote_copy(
                send_p.at[i, peer],
                recv_p.at[i, me],
                psend_sem.at[i],
                precv_sem.at[i],
                device_id={"coil": peer // frames, "frame": lax.rem(peer, frames)},
                device_id_type=MESH,
            ).start()
            return carry

        lax.fori_loop(1, owners, hand, 0)

    for i in range(planes):
        wait_bytes(recv_p, i, owners - 1, precv_sem)
        totals = [
            sum(recv_p[i, n * frames + f].astype(F32) for n in range(coils))
            for f in range(frames)
        ]
        out_k[i] = sum(weights[f, 0] * totals[f] for f in range(frames))
        out_v[i] = sum(weights[f, 1] * totals[f] for f in range(frames))

    for i in range(planes):
        wait_bytes(images, i, owners - 1, isend_sem)
        wait_bytes(send_f, i, pencils - 1, fsend_sem)
        wait_bytes(send_b, i, pencils - 1, bsend_sem)
        wait_bytes(send_p, i, owners - 1, psend_sem)
    pltpu.make_async_copy(base_blocks, base_blocks, base_send).wait()


def solution(mesh):
    coils, pencils, frames = mesh.shape["coil"], mesh.shape["pencil"], mesh.shape["frame"]

    def per_device(
        kdata, sampling, sensitivity, baseline, ktrans, plasma_volume, arterial, arterial_integral
    ):
        planes, rows, ny = ktrans.shape
        nx = sensitivity.shape[3]
        nz = kdata.shape[3]
        lines = kdata.shape[4]
        owners = coils * frames
        tabs = all_tables(nx, ny, nz, pencils)
        hbm = pl.BlockSpec(memory_space=pltpu.HBM)
        smem = pl.BlockSpec(memory_space=pltpu.SMEM)
        vmem = pl.BlockSpec(memory_space=pltpu.VMEM)
        out = jax.ShapeDtypeStruct((planes, rows, ny), F32)
        dma = pltpu.SemaphoreType.DMA
        blocks = (planes, pencils, 2 * lines, ny)
        return pl.pallas_call(
            lambda *refs: kernel((coils, pencils, frames), *refs),
            out_shape=(out, out),
            in_specs=[hbm, hbm, hbm, smem, smem] + [hbm] * 8,
            out_specs=(vmem, vmem),
            scratch_shapes=[
                pltpu.VMEM((planes, 2, rows, ny), BF16),
                pltpu.VMEM((2, planes, rows, ny), BF16),
                pltpu.VMEM((frames, planes, 2, rows, ny), BF16),
                pltpu.VMEM((planes, owners, 2, rows, ny), BF16),
                pltpu.VMEM((owners, planes, 2, rows, ny), BF16),
                pltpu.VMEM((2, planes, nx, ny), BF16),
                pltpu.VMEM((2, nz, lines, ny), BF16),
                pltpu.VMEM((nz, ny), jnp.int32),
                *[pltpu.VMEM(tab.shape, BF16) for tab in tabs],
                pltpu.VMEM(blocks, BF16),
                pltpu.VMEM(blocks, BF16),
                pltpu.VMEM((2 * nz * lines, ny), F32),
                pltpu.VMEM((2 * nz * lines, ny), BF16),
                pltpu.VMEM((2 * nz * lines, ny), BF16),
                pltpu.VMEM(blocks, BF16),
                pltpu.VMEM(blocks, BF16),
                pltpu.VMEM((planes, owners, rows, ny), BF16),
                pltpu.VMEM((planes, owners, rows, ny), BF16),
                pltpu.VMEM((frames, 2, rows, ny), F32),
                dma((4,)),
                dma((8,)),
                dma((planes,)),
                dma((planes,)),
                dma,
                dma,
                dma((planes,)),
                dma((planes,)),
                dma((planes,)),
                dma((planes,)),
                dma((planes,)),
                dma((planes,)),
                dma,
                dma,
            ],
            compiler_params=pltpu.CompilerParams(
                collective_id=0, has_side_effects=True, vmem_limit_bytes=56 * 1024 * 1024
            ),
        )(
            baseline,
            ktrans,
            plasma_volume,
            arterial,
            arterial_integral,
            sensitivity[0],
            kdata[0, 0],
            sampling[0],
            *[jnp.asarray(tab) for tab in tabs],
        )

    in_specs = (
        P("frame", "coil", None, None, "pencil", None),
        P("frame", None, None),
        P("coil", None, "pencil", None, None),
        P(None, "pencil", ("coil", "frame"), None),
        P("pencil", ("coil", "frame"), None),
        P("pencil", ("coil", "frame"), None),
        P("frame"),
        P("frame"),
    )
    out_specs = (P("pencil", ("coil", "frame"), None), P("pencil", ("coil", "frame"), None))
    return jax.shard_map(
        per_device, mesh=mesh, in_specs=in_specs, out_specs=out_specs, check_vma=False
    )
```

```python
import math

import jax
import jax.numpy as jnp
import numpy as np
from jax import lax
from jax.experimental import pallas as pl
from jax.experimental.pallas import tpu as pltpu
from jax.sharding import PartitionSpec as P

MESH = pl.DeviceIdType.MESH
F32 = jnp.float32
BF16 = jnp.bfloat16


def tables(size):
    index = np.arange(size)
    product = index[:, None] * index[None, :] % size
    angle = product.astype(np.float32) * np.float32(2.0 * math.pi / size)
    scale = np.float32(1.0 / math.sqrt(size))
    return (
        (np.cos(angle.astype(np.float64)).astype(np.float32) * scale).astype(BF16),
        (np.sin(angle.astype(np.float64)).astype(np.float32) * scale).astype(BF16),
    )


def complex_table(size):
    cos_t, sin_t = tables(size)
    return np.stack(
        [
            np.stack([cos_t.T, sin_t.T], axis=1),
            np.stack([-sin_t.T, cos_t.T], axis=1),
        ]
    )


def all_tables(nx, ny, nz, pencils):
    lines, planes = nx // pencils, nz // pencils
    cos_y, sin_y = tables(ny)
    rows_y = np.concatenate([cos_y, sin_y], axis=1)
    full_x = complex_table(nx)
    forward_x = (
        full_x.reshape(2, pencils, lines, 2 * nx)
        .transpose(1, 0, 2, 3)
        .reshape(2 * nx, 2 * nx)
    )
    inverse_x = np.ascontiguousarray(forward_x.T)
    full_z = complex_table(nz)
    spread = np.einsum(
        "akbz,ij->akibzj", full_z.astype(np.float32), np.eye(lines, dtype=np.float32)
    )
    spread = spread.reshape(2, nz, lines, 2, pencils, planes, lines)
    forward_z = (
        spread.transpose(5, 0, 1, 2, 4, 3, 6)
        .reshape(planes, 2 * nz * lines, pencils * 2 * lines)
        .astype(BF16)
    )
    inverse_z = np.ascontiguousarray(forward_z.transpose(0, 2, 1))
    return rows_y, forward_x, inverse_x, forward_z, inverse_z


def dot(a, b):
    return jnp.dot(a, b, preferred_element_type=F32)


def split(value):
    high = value.astype(BF16)
    return high, (value - high.astype(F32)).astype(BF16)


def kernel(
    sizes,
    base_in,
    ktrans_in,
    volume_in,
    arterial,
    integral,
    sens_in,
    kdata_in,
    sampling_in,
    rows_y_in,
    forward_x_in,
    inverse_x_in,
    forward_z_in,
    inverse_z_in,
    out,
    own_base,
    own_params,
    own_frames,
    images,
    bases,
    sens,
    kdata,
    sampling,
    rows_y,
    forward_x,
    inverse_x,
    forward_z,
    inverse_z,
    send_f,
    recv_f,
    kspace,
    residual,
    send_b,
    recv_b,
    send_p,
    recv_p,
    weights,
    own_sem,
    load_sem,
    isend_sem,
    irecv_sem,
    base_send,
    base_recv,
    fsend_sem,
    frecv_sem,
    bsend_sem,
    brecv_sem,
    psend_sem,
    precv_sem,
    wsend_sem,
    wrecv_sem,
):
    coils, pencils, frames = sizes
    planes, owners = images.shape[:2]
    nx, ny = sens.shape[2:]
    halves, width = send_f.shape[1], send_f.shape[-1]
    c = lax.axis_index("coil")
    p = lax.axis_index("pencil")
    t = lax.axis_index("frame")
    me = c * frames + t
    other = 1 - t

    own = [
        pltpu.make_async_copy(base_in.at[0], own_base.at[:, 0], own_sem.at[0]),
        pltpu.make_async_copy(base_in.at[1], own_base.at[:, 1], own_sem.at[1]),
        pltpu.make_async_copy(ktrans_in, own_params.at[0], own_sem.at[2]),
        pltpu.make_async_copy(volume_in, own_params.at[1], own_sem.at[3]),
    ]
    for copy in own:
        copy.start()
    barrier = pltpu.get_barrier_semaphore()

    def greet_pencil(d, carry):
        peer = lax.rem(p + d, pencils)
        pl.semaphore_signal(barrier, inc=1, device_id={"pencil": peer}, device_id_type=MESH)
        return carry

    lax.fori_loop(1, pencils, greet_pencil, 0)

    def greet_maps(d, carry):
        peer = lax.rem(me + d, coils * frames)
        pl.semaphore_signal(
            barrier,
            inc=1,
            device_id={"coil": peer // frames, "frame": lax.rem(peer, frames)},
            device_id_type=MESH,
        )
        return carry

    lax.fori_loop(1, coils * frames, greet_maps, 0)

    pairs = [
        (rows_y_in, rows_y),
        (sens_in, sens),
        (forward_x_in, forward_x),
        (forward_z_in, forward_z),
        (kdata_in, kdata),
        (sampling_in, sampling),
        (inverse_z_in, inverse_z),
        (inverse_x_in, inverse_x),
    ]
    loads = [
        pltpu.make_async_copy(src, dst, load_sem.at[n])
        for n, (src, dst) in enumerate(pairs)
    ]
    for copy in loads:
        copy.start()

    weights[t, 0] = jnp.full(weights.shape[2:], integral[0], F32)
    weights[t, 1] = jnp.full(weights.shape[2:], arterial[0], F32)

    def frame_rows(frame):
        factor = (
            1.0
            + weights[frame, 0] * own_params[0].astype(F32)
            + weights[frame, 1] * own_params[1].astype(F32)
        )
        own_frames[frame] = (own_base[...].astype(F32) * factor[:, None]).astype(BF16)

    for copy in own:
        copy.wait()
    frame_rows(t)
    pl.semaphore_wait(barrier, pencils - 1 + owners - 1)
    weight_copy = pltpu.make_async_remote_copy(
        weights.at[t],
        weights.at[t],
        wsend_sem,
        wrecv_sem,
        device_id={"frame": other},
        device_id_type=MESH,
    )
    weight_copy.start()

    def images_to(i, frame, first):
        def one(d, carry):
            peer = lax.rem(c + d, coils)
            pltpu.make_async_remote_copy(
                own_frames.at[frame, i],
                images.at[i, me],
                isend_sem.at[i],
                irecv_sem.at[i],
                device_id={"coil": peer, "frame": frame},
                device_id_type=MESH,
            ).start()
            return carry

        lax.fori_loop(first, coils, one, 0)

    def bases_to(d, carry):
        peer = lax.rem(me + d, owners)
        pltpu.make_async_remote_copy(
            own_base,
            bases.at[me],
            base_send,
            base_recv,
            device_id={"coil": peer // frames, "frame": lax.rem(peer, frames)},
            device_id_type=MESH,
        ).start()
        return carry

    def forward(i):
        shape = (nx, images.shape[-1])
        frame_re = images[i, :, 0].reshape(shape).astype(F32)
        frame_im = images[i, :, 1].reshape(shape).astype(F32)
        sens_re = sens[0, i].astype(F32)
        sens_im = sens[1, i].astype(F32)
        high, low = split(
            jnp.concatenate(
                [
                    sens_re * frame_re - sens_im * frame_im,
                    sens_re * frame_im + sens_im * frame_re,
                ],
                axis=0,
            )
        )
        y = dot(high, rows_y[...]) + dot(low, rows_y[...])
        high, low = split(
            jnp.concatenate(
                [y[:nx, :ny] + y[nx:, ny:], y[nx:, :ny] - y[:nx, ny:]], axis=0
            )
        )
        x = dot(forward_x[...], high) + dot(forward_x[...], low)
        for h in range(halves):
            cut = x[:, h * width : (h + 1) * width]
            send_f[:, h, i] = cut.astype(BF16).reshape(pencils, -1, width)
        recv_f[p, :, i] = send_f[p, :, i]
        if i < planes - 1:
            exchange(send_f, recv_f, fsend_sem, frecv_sem, i, (slice(None), i))
        else:
            for h in range(halves):
                exchange(send_f, recv_f, fsend_sem, frecv_sem, i + h, (h, i))

    def exchange(src, dst, send_sem, recv_sem, n, part):
        def one(d, carry):
            peer = lax.rem(p + d, pencils)
            pltpu.make_async_remote_copy(
                src.at[(peer, *part)],
                dst.at[(p, *part)],
                send_sem.at[n],
                recv_sem.at[n],
                device_id={"pencil": peer},
                device_id_type=MESH,
            ).start()
            return carry

        lax.fori_loop(1, pencils, one, 0)

    def all_but_one(ref, part, sem):
        view = ref.at[(pl.ds(0, pencils - 1), *part)]
        pltpu.make_async_copy(view, view, sem).wait()

    def wait_bytes(ref, i, count, sem):
        view = ref.at[i, pl.ds(0, count)]
        pltpu.make_async_copy(view, view, sem.at[i]).wait()

    images_to(0, t, 1)
    weight_copy.wait()
    frame_rows(other)
    images_to(0, other, 0)
    for i in range(1, planes):
        images_to(i, t, 1)
        images_to(i, other, 0)
    images[:, me] = own_frames[t]
    bases[me] = own_base[...]
    for copy in loads[:3]:
        copy.wait()
    for i in range(planes):
        wait_bytes(images, i, owners - 1, irecv_sem)
        forward(i)
    lax.fori_loop(1, owners, bases_to, 0)

    for copy in loads[3:6]:
        copy.wait()
    last = planes - 1
    for i in range(last):
        all_but_one(recv_f, (slice(None), i), frecv_sem.at[i])
        lines = jnp.concatenate(
            [recv_f[:, h, i].reshape(-1, width) for h in range(halves)], axis=1
        )
        if i == 0:
            so_far = -kdata[...].astype(F32).reshape(kspace.shape)
        else:
            so_far = kspace[...]
        kspace[...] = dot(forward_z[i], lines) + so_far
    loads[6].wait()
    half_rows = kspace.shape[0] // 2
    for h in range(halves):
        all_but_one(recv_f, (h, last), frecv_sem.at[last + h])
        lines = recv_f[:, h, last].reshape(-1, width)
        columns = slice(h * width, (h + 1) * width)
        keep = sampling[:, columns].astype(F32)[:, None, :]
        for part in range(2):
            rows = slice(part * half_rows, (part + 1) * half_rows)
            value = dot(forward_z[last, rows, :], lines) + kspace[rows, columns]
            value = keep * value.reshape(keep.shape[0], -1, width)
            high, low = split(value.reshape(half_rows, width))
            residual[h, rows, :width] = high
            residual[h, rows, width:] = low
        for i in range(planes):
            x = dot(inverse_z[i], residual[h])
            x = (x[:, :width] + x[:, width:]).astype(BF16)
            send_b[:, h, i] = x.reshape(pencils, -1, width)
            recv_b[p, h, i] = send_b[p, h, i]
            exchange(send_b, recv_b, bsend_sem, brecv_sem, h * planes + i, (h, i))

    loads[7].wait()
    base_blocks = bases.at[pl.ds(0, owners - 1)]
    pltpu.make_async_copy(base_blocks, base_blocks, base_recv).wait()
    for i in range(planes):
        for h in range(halves):
            all_but_one(recv_b, (h, i), brecv_sem.at[h * planes + i])
        lines = jnp.concatenate(
            [recv_b[:, h, i].reshape(-1, width) for h in range(halves)], axis=1
        )
        x = dot(inverse_x[...], lines)
        high, low = split(x)
        y = dot(high, rows_y[...]) + dot(low, rows_y[...])
        back_re = y[:nx, :ny] - y[nx:, ny:]
        back_im = y[nx:, :ny] + y[:nx, ny:]
        sens_re = sens[0, i].astype(F32)
        sens_im = sens[1, i].astype(F32)
        adj_re = sens_re * back_re + sens_im * back_im
        adj_im = sens_re * back_im - sens_im * back_re
        base_re = bases[:, i, 0].reshape(nx, ny).astype(F32)
        base_im = bases[:, i, 1].reshape(nx, ny).astype(F32)
        terms = base_re * adj_re + base_im * adj_im
        send_p[i] = terms.astype(BF16).reshape(send_p.shape[1:])
        recv_p[i, me] = send_p[i, me]

        def hand(d, carry):
            peer = lax.rem(me + d, owners)
            pltpu.make_async_remote_copy(
                send_p.at[i, peer],
                recv_p.at[i, me],
                psend_sem.at[i],
                precv_sem.at[i],
                device_id={"coil": peer // frames, "frame": lax.rem(peer, frames)},
                device_id_type=MESH,
            ).start()
            return carry

        lax.fori_loop(1, owners, hand, 0)

    for i in range(planes):
        wait_bytes(recv_p, i, owners - 1, precv_sem)
        for f in range(frames):
            out[f, i] = sum(recv_p[i, n * frames + f].astype(F32) for n in range(coils))
    for f in range(frames):
        out[f, planes, 0:1] = weights[f, 0, 0:1]
        out[f, planes, 1:2] = weights[f, 1, 0:1]

    for i in range(planes):
        wait_bytes(images, i, owners - 1, isend_sem)
        for h in range(halves):
            if i == last:
                all_but_one(send_f, (h, i), fsend_sem.at[last + h])
            all_but_one(send_b, (h, i), bsend_sem.at[h * planes + i])
        if i < last:
            all_but_one(send_f, (slice(None), i), fsend_sem.at[i])
        wait_bytes(send_p, i, owners - 1, psend_sem)
    pltpu.make_async_copy(base_blocks, base_blocks, base_send).wait()


def solution(mesh):
    coils, pencils, frames = mesh.shape["coil"], mesh.shape["pencil"], mesh.shape["frame"]

    def per_device(
        kdata, sampling, sensitivity, baseline, ktrans, plasma_volume, arterial, arterial_integral
    ):
        planes, rows, ny = ktrans.shape
        nx = sensitivity.shape[3]
        nz = kdata.shape[3]
        lines = kdata.shape[4]
        owners = coils * frames
        tabs = all_tables(nx, ny, nz, pencils)
        hbm = pl.BlockSpec(memory_space=pltpu.HBM)
        smem = pl.BlockSpec(memory_space=pltpu.SMEM)
        vmem = pl.BlockSpec(memory_space=pltpu.VMEM)
        dma = pltpu.SemaphoreType.DMA
        halves = 2 if ny % 256 == 0 else 1
        blocks = (pencils, halves, planes, 2 * lines, ny // halves)
        out = pl.pallas_call(
            lambda *refs: kernel((coils, pencils, frames), *refs),
            out_shape=jax.ShapeDtypeStruct((frames, planes + 1, rows, ny), F32),
            in_specs=[hbm, hbm, hbm, smem, smem] + [hbm] * 8,
            out_specs=vmem,
            scratch_shapes=[
                pltpu.VMEM((planes, 2, rows, ny), BF16),
                pltpu.VMEM((2, planes, rows, ny), BF16),
                pltpu.VMEM((frames, planes, 2, rows, ny), BF16),
                pltpu.VMEM((planes, owners, 2, rows, ny), BF16),
                pltpu.VMEM((owners, planes, 2, rows, ny), BF16),
                pltpu.VMEM((2, planes, nx, ny), BF16),
                pltpu.VMEM((2, nz, lines, ny), BF16),
                pltpu.VMEM((nz, ny), jnp.int32),
                *[pltpu.VMEM(tab.shape, BF16) for tab in tabs],
                pltpu.VMEM(blocks, BF16),
                pltpu.VMEM(blocks, BF16),
                pltpu.VMEM((2 * nz * lines, ny), F32),
                pltpu.VMEM((halves, 2 * nz * lines, 2 * ny // halves), BF16),
                pltpu.VMEM(blocks, BF16),
                pltpu.VMEM(blocks, BF16),
                pltpu.VMEM((planes, owners, rows, ny), BF16),
                pltpu.VMEM((planes, owners, rows, ny), BF16),
                pltpu.VMEM((frames, 2, rows, ny), F32),
                dma((4,)),
                dma((8,)),
                dma((planes,)),
                dma((planes,)),
                dma,
                dma,
                dma((planes - 1 + halves,)),
                dma((planes - 1 + halves,)),
                dma((planes * halves,)),
                dma((planes * halves,)),
                dma((planes,)),
                dma((planes,)),
                dma,
                dma,
            ],
            compiler_params=pltpu.CompilerParams(
                collective_id=0, has_side_effects=True, vmem_limit_bytes=56 * 1024 * 1024
            ),
        )(
            baseline,
            ktrans,
            plasma_volume,
            arterial,
            arterial_integral,
            sensitivity[0],
            kdata[0, 0],
            sampling[0],
            *[jnp.asarray(tab) for tab in tabs],
        )
        weights = out[:, planes, :2, 0]
        return tuple(
            sum(weights[f, n] * out[f, :planes] for f in range(frames)) for n in range(2)
        )

    in_specs = (
        P("frame", "coil", None, None, "pencil", None),
        P("frame", None, None),
        P("coil", None, "pencil", None, None),
        P(None, "pencil", ("coil", "frame"), None),
        P("pencil", ("coil", "frame"), None),
        P("pencil", ("coil", "frame"), None),
        P("frame"),
        P("frame"),
    )
    out_specs = (P("pencil", ("coil", "frame"), None), P("pencil", ("coil", "frame"), None))
    return jax.shard_map(
        per_device, mesh=mesh, in_specs=in_specs, out_specs=out_specs, check_vma=False
    )
```

```python
import math

import jax
import jax.numpy as jnp
import numpy as np
from jax import lax
from jax.experimental import pallas as pl
from jax.experimental.pallas import tpu as pltpu
from jax.sharding import PartitionSpec as P

MESH = pl.DeviceIdType.MESH
F32 = jnp.float32
BF16 = jnp.bfloat16


def tables(size):
    index = np.arange(size)
    product = index[:, None] * index[None, :] % size
    angle = product.astype(np.float32) * np.float32(2.0 * math.pi / size)
    scale = np.float32(1.0 / math.sqrt(size))
    return (
        (np.cos(angle.astype(np.float64)).astype(np.float32) * scale).astype(BF16),
        (np.sin(angle.astype(np.float64)).astype(np.float32) * scale).astype(BF16),
    )


def complex_table(size):
    cos_t, sin_t = tables(size)
    return np.stack(
        [
            np.stack([cos_t.T, sin_t.T], axis=1),
            np.stack([-sin_t.T, cos_t.T], axis=1),
        ]
    )


def all_tables(nx, ny, nz, pencils):
    lines, planes = nx // pencils, nz // pencils
    cos_y, sin_y = tables(ny)
    rows_y = np.concatenate([cos_y, sin_y], axis=1)
    full_x = complex_table(nx)
    forward_x = (
        full_x.reshape(2, pencils, lines, 2 * nx)
        .transpose(1, 0, 2, 3)
        .reshape(2 * nx, 2 * nx)
    )
    inverse_x = np.ascontiguousarray(forward_x.T)
    full_z = complex_table(nz)
    spread = np.einsum(
        "akbz,ij->akibzj", full_z.astype(np.float32), np.eye(lines, dtype=np.float32)
    )
    spread = spread.reshape(2, nz, lines, 2, pencils, planes, lines)
    forward_z = (
        spread.transpose(5, 0, 1, 2, 4, 3, 6)
        .reshape(planes, 2 * nz * lines, pencils * 2 * lines)
        .astype(BF16)
    )
    inverse_z = np.ascontiguousarray(forward_z.transpose(0, 2, 1))
    return rows_y, forward_x, inverse_x, forward_z, inverse_z


def dot(a, b):
    return jnp.dot(a, b, preferred_element_type=F32)


def split(value):
    high = value.astype(BF16)
    return high, (value - high.astype(F32)).astype(BF16)


def kernel(
    sizes,
    base_in,
    ktrans_in,
    volume_in,
    arterial,
    integral,
    sens_in,
    kdata_in,
    sampling_in,
    rows_y_in,
    forward_x_in,
    inverse_x_in,
    forward_z_in,
    inverse_z_in,
    out,
    own_base,
    own_params,
    own_frames,
    images,
    bases,
    sens,
    kdata,
    sampling,
    rows_y,
    forward_x,
    inverse_x,
    forward_z,
    inverse_z,
    send_f,
    recv_f,
    kspace,
    residual,
    send_b,
    recv_b,
    send_p,
    recv_p,
    weights,
    own_sem,
    load_sem,
    isend_sem,
    irecv_sem,
    relay_sem,
    base_send,
    base_recv,
    fsend_sem,
    frecv_sem,
    bsend_sem,
    brecv_sem,
    psend_sem,
    precv_sem,
    wsend_sem,
    wrecv_sem,
):
    coils, pencils, frames = sizes
    planes, owners = images.shape[:2]
    nx, ny = sens.shape[2:]
    halves, width = send_f.shape[1], send_f.shape[-1]
    c = lax.axis_index("coil")
    p = lax.axis_index("pencil")
    t = lax.axis_index("frame")
    me = c * frames + t
    other = 1 - t

    own = [
        pltpu.make_async_copy(base_in.at[0], own_base.at[:, 0], own_sem.at[0]),
        pltpu.make_async_copy(base_in.at[1], own_base.at[:, 1], own_sem.at[1]),
        pltpu.make_async_copy(ktrans_in, own_params.at[0], own_sem.at[2]),
        pltpu.make_async_copy(volume_in, own_params.at[1], own_sem.at[3]),
    ]
    for copy in own:
        copy.start()
    barrier = pltpu.get_barrier_semaphore()

    def greet_pencil(d, carry):
        peer = lax.rem(p + d, pencils)
        pl.semaphore_signal(barrier, inc=1, device_id={"pencil": peer}, device_id_type=MESH)
        return carry

    lax.fori_loop(1, pencils, greet_pencil, 0)

    def greet_maps(d, carry):
        peer = lax.rem(me + d, coils * frames)
        pl.semaphore_signal(
            barrier,
            inc=1,
            device_id={"coil": peer // frames, "frame": lax.rem(peer, frames)},
            device_id_type=MESH,
        )
        return carry

    lax.fori_loop(1, coils * frames, greet_maps, 0)

    pairs = [
        (rows_y_in, rows_y),
        (sens_in, sens),
        (forward_x_in, forward_x),
        (forward_z_in, forward_z),
        (kdata_in, kdata),
        (sampling_in, sampling),
        (inverse_z_in, inverse_z),
        (inverse_x_in, inverse_x),
    ]
    loads = [
        pltpu.make_async_copy(src, dst, load_sem.at[n])
        for n, (src, dst) in enumerate(pairs)
    ]
    for copy in loads:
        copy.start()

    weights[t, 0] = jnp.full(weights.shape[2:], integral[0], F32)
    weights[t, 1] = jnp.full(weights.shape[2:], arterial[0], F32)

    def frame_rows(frame):
        factor = (
            1.0
            + weights[frame, 0] * own_params[0].astype(F32)
            + weights[frame, 1] * own_params[1].astype(F32)
        )
        own_frames[frame] = (own_base[...].astype(F32) * factor[:, None]).astype(BF16)

    for copy in own:
        copy.wait()
    frame_rows(t)
    pl.semaphore_wait(barrier, pencils - 1 + owners - 1)
    weight_copy = pltpu.make_async_remote_copy(
        weights.at[t],
        weights.at[t],
        wsend_sem,
        wrecv_sem,
        device_id={"frame": other},
        device_id_type=MESH,
    )
    weight_copy.start()

    def image_copy(block, i, sem, coil, frame):
        pltpu.make_async_remote_copy(
            block,
            images.at[i, me] if frame is not None else block,
            isend_sem.at[i],
            sem,
            device_id={"coil": lax.rem(coil + coils, coils)}
            | ({} if frame is None else {"frame": frame}),
            device_id_type=MESH,
        ).start()

    def images_to(i, frame):
        block = own_frames.at[frame, i]
        image_copy(block, i, relay_sem.at[i, t, 0], c + 2, frame)
        image_copy(block, i, relay_sem.at[i, t, 1], c - 2, frame)
        image_copy(block, i, irecv_sem.at[i], c + 1, frame)
        image_copy(block, i, irecv_sem.at[i], c - 1, frame)
        if frame is other:
            image_copy(block, i, irecv_sem.at[i], c, frame)

    def relay(i):
        for way, step in ((0, 1), (1, -1)):
            for frame in (t, other):
                block = images.at[
                    i, lax.rem(c - 2 * step + coils, coils) * frames + frame
                ]
                pltpu.make_async_copy(block, block, relay_sem.at[i, frame, way]).wait()
                image_copy(block, i, irecv_sem.at[i], c + step, None)
                if (way == 0) == (frame is t):
                    image_copy(block, i, irecv_sem.at[i], c + 2 * step, None)

    def bases_to(d, carry):
        peer = lax.rem(me + d, owners)
        pltpu.make_async_remote_copy(
            own_base,
            bases.at[me],
            base_send,
            base_recv,
            device_id={"coil": peer // frames, "frame": lax.rem(peer, frames)},
            device_id_type=MESH,
        ).start()
        return carry

    slabs = [(h, i) for h in range(halves) for i in range(1, planes)]
    parts = [(slice(None), 0), *slabs]

    def send_forward(n):
        exchange(send_f, recv_f, fsend_sem, frecv_sem, n, parts[n])

    def forward(i):
        shape = (nx, images.shape[-1])
        frame_re = images[i, :, 0].reshape(shape).astype(F32)
        frame_im = images[i, :, 1].reshape(shape).astype(F32)
        sens_re = sens[0, i].astype(F32)
        sens_im = sens[1, i].astype(F32)
        high, low = split(
            jnp.concatenate(
                [
                    sens_re * frame_re - sens_im * frame_im,
                    sens_re * frame_im + sens_im * frame_re,
                ],
                axis=0,
            )
        )
        y = dot(high, rows_y[...]) + dot(low, rows_y[...])
        high, low = split(
            jnp.concatenate(
                [y[:nx, :ny] + y[nx:, ny:], y[nx:, :ny] - y[:nx, ny:]], axis=0
            )
        )
        x = dot(forward_x[...], high) + dot(forward_x[...], low)
        for h in range(halves):
            cut = x[:, h * width : (h + 1) * width]
            send_f[:, h, i] = cut.astype(BF16).reshape(pencils, -1, width)
        recv_f[p, :, i] = send_f[p, :, i]
        if i == 0:
            send_forward(0)
        else:
            send_forward(1 + slabs.index((0, i)))
        if i == planes - 1:
            for n in range(planes, len(slabs) + 1):
                send_forward(n)

    def exchange(src, dst, send_sem, recv_sem, n, part):
        def one(d, carry):
            peer = lax.rem(p + d, pencils)
            pltpu.make_async_remote_copy(
                src.at[(peer, *part)],
                dst.at[(p, *part)],
                send_sem.at[n],
                recv_sem.at[n],
                device_id={"pencil": peer},
                device_id_type=MESH,
            ).start()
            return carry

        lax.fori_loop(1, pencils, one, 0)

    def all_but_one(ref, part, sem):
        view = ref.at[(pl.ds(0, pencils - 1), *part)]
        pltpu.make_async_copy(view, view, sem).wait()

    def wait_bytes(ref, i, count, sem):
        view = ref.at[i, pl.ds(0, count)]
        pltpu.make_async_copy(view, view, sem.at[i]).wait()

    images_to(0, t)
    images_to(1, t)
    weight_copy.wait()
    frame_rows(other)
    images_to(0, other)
    images_to(1, other)
    for i in range(2, planes):
        images_to(i, t)
        images_to(i, other)
    images[:, me] = own_frames[t]
    bases[me] = own_base[...]
    for copy in loads[:3]:
        copy.wait()
    relay(0)
    for i in range(planes):
        if i < planes - 1:
            relay(i + 1)
        wait_bytes(images, i, owners - 5, irecv_sem)
        forward(i)
    lax.fori_loop(1, owners, bases_to, 0)

    for copy in loads[3:6]:
        copy.wait()
    all_but_one(recv_f, parts[0], frecv_sem.at[0])
    lines = jnp.concatenate(
        [recv_f[:, h, 0].reshape(-1, width) for h in range(halves)], axis=1
    )
    kspace[...] = dot(forward_z[0], lines) - kdata[...].astype(F32).reshape(kspace.shape)
    loads[6].wait()
    half_rows = kspace.shape[0] // 2
    for h in range(halves):
        columns = slice(h * width, (h + 1) * width)
        for i in range(1, planes):
            all_but_one(recv_f, (h, i), frecv_sem.at[1 + slabs.index((h, i))])
            lines = recv_f[:, h, i].reshape(-1, width)
            if i < planes - 1:
                kspace[:, columns] = dot(forward_z[i], lines) + kspace[:, columns]
        keep = sampling[:, columns].astype(F32)[:, None, :]
        for part in range(2):
            rows = slice(part * half_rows, (part + 1) * half_rows)
            value = dot(forward_z[planes - 1, rows, :], lines) + kspace[rows, columns]
            value = keep * value.reshape(keep.shape[0], -1, width)
            high, low = split(value.reshape(half_rows, width))
            residual[h, rows, :width] = high
            residual[h, rows, width:] = low
        for i in range(planes):
            x = dot(inverse_z[i], residual[h])
            x = (x[:, :width] + x[:, width:]).astype(BF16)
            send_b[:, h, i] = x.reshape(pencils, -1, width)
            recv_b[p, h, i] = send_b[p, h, i]
            exchange(send_b, recv_b, bsend_sem, brecv_sem, h * planes + i, (h, i))

    loads[7].wait()
    base_blocks = bases.at[pl.ds(0, owners - 1)]
    pltpu.make_async_copy(base_blocks, base_blocks, base_recv).wait()
    for i in range(planes):
        for h in range(halves):
            all_but_one(recv_b, (h, i), brecv_sem.at[h * planes + i])
        lines = jnp.concatenate(
            [recv_b[:, h, i].reshape(-1, width) for h in range(halves)], axis=1
        )
        x = dot(inverse_x[...], lines)
        high, low = split(x)
        y = dot(high, rows_y[...]) + dot(low, rows_y[...])
        back_re = y[:nx, :ny] - y[nx:, ny:]
        back_im = y[nx:, :ny] + y[:nx, ny:]
        sens_re = sens[0, i].astype(F32)
        sens_im = sens[1, i].astype(F32)
        adj_re = sens_re * back_re + sens_im * back_im
        adj_im = sens_re * back_im - sens_im * back_re
        base_re = bases[:, i, 0].reshape(nx, ny).astype(F32)
        base_im = bases[:, i, 1].reshape(nx, ny).astype(F32)
        terms = base_re * adj_re + base_im * adj_im
        send_p[i] = terms.astype(BF16).reshape(send_p.shape[1:])
        recv_p[i, me] = send_p[i, me]

        def hand(d, carry):
            peer = lax.rem(me + d, owners)
            pltpu.make_async_remote_copy(
                send_p.at[i, peer],
                recv_p.at[i, me],
                psend_sem.at[i],
                precv_sem.at[i],
                device_id={"coil": peer // frames, "frame": lax.rem(peer, frames)},
                device_id_type=MESH,
            ).start()
            return carry

        lax.fori_loop(1, owners, hand, 0)

    for i in range(planes):
        wait_bytes(recv_p, i, owners - 1, precv_sem)
        for f in range(frames):
            total = sum(recv_p[i, n * frames + f].astype(F32) for n in range(coils))
            for n in range(2):
                out[n, f, i] = weights[f, n] * total

    for i in range(planes):
        wait_bytes(images, i, owners - 1, isend_sem)
        for h in range(halves):
            all_but_one(send_b, (h, i), bsend_sem.at[h * planes + i])
        wait_bytes(send_p, i, owners - 1, psend_sem)
    for n, part in enumerate(parts):
        all_but_one(send_f, part, fsend_sem.at[n])
    pltpu.make_async_copy(base_blocks, base_blocks, base_send).wait()


def solution(mesh):
    coils, pencils, frames = mesh.shape["coil"], mesh.shape["pencil"], mesh.shape["frame"]

    def per_device(
        kdata, sampling, sensitivity, baseline, ktrans, plasma_volume, arterial, arterial_integral
    ):
        planes, rows, ny = ktrans.shape
        nx = sensitivity.shape[3]
        nz = kdata.shape[3]
        lines = kdata.shape[4]
        owners = coils * frames
        tabs = all_tables(nx, ny, nz, pencils)
        hbm = pl.BlockSpec(memory_space=pltpu.HBM)
        smem = pl.BlockSpec(memory_space=pltpu.SMEM)
        vmem = pl.BlockSpec(memory_space=pltpu.VMEM)
        dma = pltpu.SemaphoreType.DMA
        halves = 2 if ny % 256 == 0 else 1
        blocks = (pencils, halves, planes, 2 * lines, ny // halves)
        out = pl.pallas_call(
            lambda *refs: kernel((coils, pencils, frames), *refs),
            out_shape=jax.ShapeDtypeStruct((2, frames, planes, rows, ny), F32),
            in_specs=[hbm, hbm, hbm, smem, smem] + [hbm] * 8,
            out_specs=vmem,
            scratch_shapes=[
                pltpu.VMEM((planes, 2, rows, ny), BF16),
                pltpu.VMEM((2, planes, rows, ny), BF16),
                pltpu.VMEM((frames, planes, 2, rows, ny), BF16),
                pltpu.VMEM((planes, owners, 2, rows, ny), BF16),
                pltpu.VMEM((owners, planes, 2, rows, ny), BF16),
                pltpu.VMEM((2, planes, nx, ny), BF16),
                pltpu.VMEM((2, nz, lines, ny), BF16),
                pltpu.VMEM((nz, ny), jnp.int32),
                *[pltpu.VMEM(tab.shape, BF16) for tab in tabs],
                pltpu.VMEM(blocks, BF16),
                pltpu.VMEM(blocks, BF16),
                pltpu.VMEM((2 * nz * lines, ny), F32),
                pltpu.VMEM((halves, 2 * nz * lines, 2 * ny // halves), BF16),
                pltpu.VMEM(blocks, BF16),
                pltpu.VMEM(blocks, BF16),
                pltpu.VMEM((planes, owners, rows, ny), BF16),
                pltpu.VMEM((planes, owners, rows, ny), BF16),
                pltpu.VMEM((frames, 2, rows, ny), F32),
                dma((4,)),
                dma((8,)),
                dma((planes,)),
                dma((planes,)),
                dma((planes, frames, 2)),
                dma,
                dma,
                dma((1 + halves * (planes - 1),)),
                dma((1 + halves * (planes - 1),)),
                dma((planes * halves,)),
                dma((planes * halves,)),
                dma((planes,)),
                dma((planes,)),
                dma,
                dma,
            ],
            compiler_params=pltpu.CompilerParams(
                collective_id=0, has_side_effects=True, vmem_limit_bytes=56 * 1024 * 1024
            ),
        )(
            baseline,
            ktrans,
            plasma_volume,
            arterial,
            arterial_integral,
            sensitivity[0],
            kdata[0, 0],
            sampling[0],
            *[jnp.asarray(tab) for tab in tabs],
        )
        return tuple(sum(out[n, f] for f in range(frames)) for n in range(2))

    in_specs = (
        P("frame", "coil", None, None, "pencil", None),
        P("frame", None, None),
        P("coil", None, "pencil", None, None),
        P(None, "pencil", ("coil", "frame"), None),
        P("pencil", ("coil", "frame"), None),
        P("pencil", ("coil", "frame"), None),
        P("frame"),
        P("frame"),
    )
    out_specs = (P("pencil", ("coil", "frame"), None), P("pencil", ("coil", "frame"), None))
    return jax.shard_map(
        per_device, mesh=mesh, in_specs=in_specs, out_specs=out_specs, check_vma=False
    )
```

```python
import math

import jax
import jax.numpy as jnp
import numpy as np
from jax import lax
from jax.experimental import pallas as pl
from jax.experimental.pallas import tpu as pltpu
from jax.sharding import PartitionSpec as P

MESH = pl.DeviceIdType.MESH
F32 = jnp.float32
BF16 = jnp.bfloat16


def tables(size):
    index = np.arange(size)
    product = index[:, None] * index[None, :] % size
    angle = product.astype(np.float32) * np.float32(2.0 * math.pi / size)
    scale = np.float32(1.0 / math.sqrt(size))
    return (
        (np.cos(angle.astype(np.float64)).astype(np.float32) * scale).astype(BF16),
        (np.sin(angle.astype(np.float64)).astype(np.float32) * scale).astype(BF16),
    )


def complex_table(size):
    cos_t, sin_t = tables(size)
    return np.stack(
        [
            np.stack([cos_t.T, sin_t.T], axis=1),
            np.stack([-sin_t.T, cos_t.T], axis=1),
        ]
    )


def all_tables(nx, ny, nz, pencils):
    lines, planes = nx // pencils, nz // pencils
    cos_y, sin_y = tables(ny)
    rows_y = np.concatenate([cos_y, sin_y], axis=1)
    full_x = complex_table(nx)
    forward_x = (
        full_x.reshape(2, pencils, lines, 2 * nx)
        .transpose(1, 0, 2, 3)
        .reshape(2 * nx, 2 * nx)
    )
    inverse_x = np.ascontiguousarray(forward_x.T)
    full_z = complex_table(nz)
    spread = np.einsum(
        "akbz,ij->akibzj", full_z.astype(np.float32), np.eye(lines, dtype=np.float32)
    )
    spread = spread.reshape(2, nz, lines, 2, pencils, planes, lines)
    forward_z = (
        spread.transpose(5, 0, 1, 2, 4, 3, 6)
        .reshape(planes, 2 * nz * lines, pencils * 2 * lines)
        .astype(BF16)
    )
    inverse_z = np.ascontiguousarray(forward_z.transpose(0, 2, 1))
    return rows_y, forward_x, inverse_x, forward_z, inverse_z


def dot(a, b):
    return jnp.dot(a, b, preferred_element_type=F32)


def split(value):
    high = value.astype(BF16)
    return high, (value - high.astype(F32)).astype(BF16)


def kernel(
    sizes,
    base_in,
    ktrans_in,
    volume_in,
    arterial,
    integral,
    sens_in,
    kdata_in,
    sampling_in,
    rows_y_in,
    forward_x_in,
    inverse_x_in,
    forward_z_in,
    inverse_z_in,
    out,
    own_base,
    own_params,
    own_frames,
    images,
    bases,
    sens,
    kdata,
    sampling,
    rows_y,
    forward_x,
    inverse_x,
    forward_z,
    inverse_z,
    send_f,
    recv_f,
    kspace,
    residual,
    send_b,
    recv_b,
    send_p,
    recv_p,
    weights,
    own_sem,
    load_sem,
    isend_sem,
    irecv_sem,
    relay_sem,
    base_send,
    base_recv,
    fsend_sem,
    frecv_sem,
    bsend_sem,
    brecv_sem,
    psend_sem,
    precv_sem,
    wsend_sem,
    wrecv_sem,
):
    coils, pencils, frames = sizes
    planes, owners = images.shape[:2]
    nx, ny = sens.shape[2:]
    halves, width = send_f.shape[1], send_f.shape[-1]
    c = lax.axis_index("coil")
    p = lax.axis_index("pencil")
    t = lax.axis_index("frame")
    me = c * frames + t
    other = 1 - t

    own = [
        pltpu.make_async_copy(base_in.at[0], own_base.at[:, 0], own_sem.at[0]),
        pltpu.make_async_copy(base_in.at[1], own_base.at[:, 1], own_sem.at[1]),
        pltpu.make_async_copy(ktrans_in, own_params.at[0], own_sem.at[2]),
        pltpu.make_async_copy(volume_in, own_params.at[1], own_sem.at[3]),
    ]
    for copy in own:
        copy.start()
    barrier = pltpu.get_barrier_semaphore()

    def greet_pencil(d, carry):
        peer = lax.rem(p + d, pencils)
        pl.semaphore_signal(barrier, inc=1, device_id={"pencil": peer}, device_id_type=MESH)
        return carry

    lax.fori_loop(1, pencils, greet_pencil, 0)

    def greet_maps(d, carry):
        peer = lax.rem(me + d, coils * frames)
        pl.semaphore_signal(
            barrier,
            inc=1,
            device_id={"coil": peer // frames, "frame": lax.rem(peer, frames)},
            device_id_type=MESH,
        )
        return carry

    lax.fori_loop(1, coils * frames, greet_maps, 0)

    pairs = [
        (rows_y_in, rows_y),
        (sens_in, sens),
        (forward_x_in, forward_x),
        (forward_z_in, forward_z),
        (kdata_in, kdata),
        (sampling_in, sampling),
        (inverse_z_in, inverse_z),
        (inverse_x_in, inverse_x),
    ]
    loads = [
        pltpu.make_async_copy(src, dst, load_sem.at[n])
        for n, (src, dst) in enumerate(pairs)
    ]
    for copy in loads:
        copy.start()

    weights[t, 0] = jnp.full(weights.shape[2:], integral[0], F32)
    weights[t, 1] = jnp.full(weights.shape[2:], arterial[0], F32)

    def frame_rows(frame):
        factor = (
            1.0
            + weights[frame, 0] * own_params[0].astype(F32)
            + weights[frame, 1] * own_params[1].astype(F32)
        )
        own_frames[frame] = (own_base[...].astype(F32) * factor[:, None]).astype(BF16)

    for copy in own:
        copy.wait()
    frame_rows(t)
    pl.semaphore_wait(barrier, pencils - 1 + owners - 1)
    weight_copy = pltpu.make_async_remote_copy(
        weights.at[t],
        weights.at[t],
        wsend_sem,
        wrecv_sem,
        device_id={"frame": other},
        device_id_type=MESH,
    )
    weight_copy.start()

    def image_copy(block, i, sem, coil, frame):
        pltpu.make_async_remote_copy(
            block,
            images.at[i, me] if frame is not None else block,
            isend_sem.at[i],
            sem,
            device_id={"coil": lax.rem(coil + coils, coils)}
            | ({} if frame is None else {"frame": frame}),
            device_id_type=MESH,
        ).start()

    def images_to(i, frame):
        block = own_frames.at[frame, i]
        image_copy(block, i, relay_sem.at[i, t, 0], c + 2, frame)
        image_copy(block, i, relay_sem.at[i, t, 1], c - 2, frame)
        image_copy(block, i, irecv_sem.at[i], c + 1, frame)
        image_copy(block, i, irecv_sem.at[i], c - 1, frame)
        if frame is other:
            image_copy(block, i, irecv_sem.at[i], c, frame)

    def relay(i):
        for way, step in ((0, 1), (1, -1)):
            for frame in (t, other):
                block = images.at[
                    i, lax.rem(c - 2 * step + coils, coils) * frames + frame
                ]
                pltpu.make_async_copy(block, block, relay_sem.at[i, frame, way]).wait()
                image_copy(block, i, irecv_sem.at[i], c + step, None)
                if (way == 0) == (frame is t):
                    image_copy(block, i, irecv_sem.at[i], c + 2 * step, None)

    def bases_to(d, carry):
        peer = lax.rem(me + d, owners)
        pltpu.make_async_remote_copy(
            own_base,
            bases.at[me],
            base_send,
            base_recv,
            device_id={"coil": peer // frames, "frame": lax.rem(peer, frames)},
            device_id_type=MESH,
        ).start()
        return carry

    slabs = [(h, i) for h in range(halves) for i in range(1, planes)]
    parts = [(slice(None), 0), *slabs]

    def send_forward(n):
        exchange(send_f, recv_f, fsend_sem, frecv_sem, n, parts[n])

    def send_left(n):
        all_but_one(send_f, parts[n], fsend_sem.at[n])

    def forward(i):
        shape = (nx, images.shape[-1])
        frame_re = images[i, :, 0].reshape(shape).astype(F32)
        frame_im = images[i, :, 1].reshape(shape).astype(F32)
        sens_re = sens[0, i].astype(F32)
        sens_im = sens[1, i].astype(F32)
        high, low = split(
            jnp.concatenate(
                [
                    sens_re * frame_re - sens_im * frame_im,
                    sens_re * frame_im + sens_im * frame_re,
                ],
                axis=0,
            )
        )
        y = dot(high, rows_y[...]) + dot(low, rows_y[...])
        high, low = split(
            jnp.concatenate(
                [y[:nx, :ny] + y[nx:, ny:], y[nx:, :ny] - y[:nx, ny:]], axis=0
            )
        )
        x = dot(forward_x[...], high) + dot(forward_x[...], low)
        for h in range(halves):
            cut = x[:, h * width : (h + 1) * width]
            send_f[:, h, i] = cut.astype(BF16).reshape(pencils, -1, width)
        recv_f[p, :, i] = send_f[p, :, i]
        send_forward(i)

    def exchange(src, dst, send_sem, recv_sem, n, part):
        def one(d, carry):
            peer = lax.rem(p + d, pencils)
            pltpu.make_async_remote_copy(
                src.at[(peer, *part)],
                dst.at[(p, *part)],
                send_sem.at[n],
                recv_sem.at[n],
                device_id={"pencil": peer},
                device_id_type=MESH,
            ).start()
            return carry

        lax.fori_loop(1, pencils, one, 0)

    def all_but_one(ref, part, sem):
        view = ref.at[(pl.ds(0, pencils - 1), *part)]
        pltpu.make_async_copy(view, view, sem).wait()

    def wait_bytes(ref, i, count, sem):
        view = ref.at[i, pl.ds(0, count)]
        pltpu.make_async_copy(view, view, sem.at[i]).wait()

    images_to(0, t)
    weight_copy.wait()
    frame_rows(other)
    images_to(0, other)
    images[:, me] = own_frames[t]
    bases[me] = own_base[...]
    for copy in loads[:3]:
        copy.wait()
    for i in range(planes):
        relay(i)
        if i < planes - 1:
            images_to(i + 1, t)
            images_to(i + 1, other)
        wait_bytes(images, i, owners - 5, irecv_sem)
        forward(i)
    lax.fori_loop(1, owners, bases_to, 0)

    for copy in loads[3:6]:
        copy.wait()
    for n in range(planes, len(parts)):
        if n == len(parts) - 1:
            all_but_one(recv_f, parts[0], frecv_sem.at[0])
            lines = jnp.concatenate(
                [recv_f[:, h, 0].reshape(-1, width) for h in range(halves)], axis=1
            )
            measured = kdata[...].astype(F32).reshape(kspace.shape)
            kspace[...] = dot(forward_z[0], lines) - measured
        send_left(n - 2)
        send_forward(n)
    loads[6].wait()
    half_rows = kspace.shape[0] // 2

    def sent_back(n):
        all_but_one(send_b, (n // planes, n % planes), bsend_sem.at[n])

    for h in range(halves):
        columns = slice(h * width, (h + 1) * width)
        for i in range(1, planes):
            all_but_one(recv_f, (h, i), frecv_sem.at[1 + slabs.index((h, i))])
            lines = recv_f[:, h, i].reshape(-1, width)
            if i < planes - 1:
                kspace[:, columns] = dot(forward_z[i], lines) + kspace[:, columns]
        keep = sampling[:, columns].astype(F32)[:, None, :]
        for part in range(2):
            rows = slice(part * half_rows, (part + 1) * half_rows)
            value = dot(forward_z[planes - 1, rows, :], lines) + kspace[rows, columns]
            value = keep * value.reshape(keep.shape[0], -1, width)
            high, low = split(value.reshape(half_rows, width))
            residual[h, rows, :width] = high
            residual[h, rows, width:] = low
        for i in range(planes):
            x = dot(inverse_z[i], residual[h])
            x = (x[:, :width] + x[:, width:]).astype(BF16)
            send_b[:, h, i] = x.reshape(pencils, -1, width)
            recv_b[p, h, i] = send_b[p, h, i]
            n = h * planes + i
            if n >= 2:
                sent_back(n - 2)
            exchange(send_b, recv_b, bsend_sem, brecv_sem, n, (h, i))

    loads[7].wait()
    base_blocks = bases.at[pl.ds(0, owners - 1)]
    pltpu.make_async_copy(base_blocks, base_blocks, base_recv).wait()
    for i in range(planes):
        for h in range(halves):
            all_but_one(recv_b, (h, i), brecv_sem.at[h * planes + i])
        lines = jnp.concatenate(
            [recv_b[:, h, i].reshape(-1, width) for h in range(halves)], axis=1
        )
        x = dot(inverse_x[...], lines)
        high, low = split(x)
        y = dot(high, rows_y[...]) + dot(low, rows_y[...])
        back_re = y[:nx, :ny] - y[nx:, ny:]
        back_im = y[nx:, :ny] + y[:nx, ny:]
        sens_re = sens[0, i].astype(F32)
        sens_im = sens[1, i].astype(F32)
        adj_re = sens_re * back_re + sens_im * back_im
        adj_im = sens_re * back_im - sens_im * back_re
        base_re = bases[:, i, 0].reshape(nx, ny).astype(F32)
        base_im = bases[:, i, 1].reshape(nx, ny).astype(F32)
        terms = base_re * adj_re + base_im * adj_im
        send_p[i] = terms.astype(BF16).reshape(send_p.shape[1:])
        recv_p[i, me] = send_p[i, me]

        def hand(d, carry):
            peer = lax.rem(me + d, owners)
            pltpu.make_async_remote_copy(
                send_p.at[i, peer],
                recv_p.at[i, me],
                psend_sem.at[i],
                precv_sem.at[i],
                device_id={"coil": peer // frames, "frame": lax.rem(peer, frames)},
                device_id_type=MESH,
            ).start()
            return carry

        lax.fori_loop(1, owners, hand, 0)

    for i in range(planes):
        wait_bytes(recv_p, i, owners - 1, precv_sem)
        for f in range(frames):
            total = sum(recv_p[i, n * frames + f].astype(F32) for n in range(coils))
            for n in range(2):
                out[n, f, i] = weights[f, n] * total

    for i in range(planes):
        wait_bytes(images, i, owners - 1, isend_sem)
        wait_bytes(send_p, i, owners - 1, psend_sem)
    for n in (*range(planes - 2), len(parts) - 2, len(parts) - 1):
        send_left(n)
    for n in range(halves * planes - 2, halves * planes):
        sent_back(n)
    pltpu.make_async_copy(base_blocks, base_blocks, base_send).wait()


def solution(mesh):
    coils, pencils, frames = mesh.shape["coil"], mesh.shape["pencil"], mesh.shape["frame"]

    def per_device(
        kdata, sampling, sensitivity, baseline, ktrans, plasma_volume, arterial, arterial_integral
    ):
        planes, rows, ny = ktrans.shape
        nx = sensitivity.shape[3]
        nz = kdata.shape[3]
        lines = kdata.shape[4]
        owners = coils * frames
        tabs = all_tables(nx, ny, nz, pencils)
        hbm = pl.BlockSpec(memory_space=pltpu.HBM)
        smem = pl.BlockSpec(memory_space=pltpu.SMEM)
        vmem = pl.BlockSpec(memory_space=pltpu.VMEM)
        dma = pltpu.SemaphoreType.DMA
        halves = 2 if ny % 256 == 0 else 1
        blocks = (pencils, halves, planes, 2 * lines, ny // halves)
        out = pl.pallas_call(
            lambda *refs: kernel((coils, pencils, frames), *refs),
            out_shape=jax.ShapeDtypeStruct((2, frames, planes, rows, ny), F32),
            in_specs=[hbm, hbm, hbm, smem, smem] + [hbm] * 8,
            out_specs=vmem,
            scratch_shapes=[
                pltpu.VMEM((planes, 2, rows, ny), BF16),
                pltpu.VMEM((2, planes, rows, ny), BF16),
                pltpu.VMEM((frames, planes, 2, rows, ny), BF16),
                pltpu.VMEM((planes, owners, 2, rows, ny), BF16),
                pltpu.VMEM((owners, planes, 2, rows, ny), BF16),
                pltpu.VMEM((2, planes, nx, ny), BF16),
                pltpu.VMEM((2, nz, lines, ny), BF16),
                pltpu.VMEM((nz, ny), jnp.int32),
                *[pltpu.VMEM(tab.shape, BF16) for tab in tabs],
                pltpu.VMEM(blocks, BF16),
                pltpu.VMEM(blocks, BF16),
                pltpu.VMEM((2 * nz * lines, ny), F32),
                pltpu.VMEM((halves, 2 * nz * lines, 2 * ny // halves), BF16),
                pltpu.VMEM(blocks, BF16),
                pltpu.VMEM(blocks, BF16),
                pltpu.VMEM((planes, owners, rows, ny), BF16),
                pltpu.VMEM((planes, owners, rows, ny), BF16),
                pltpu.VMEM((frames, 2, rows, ny), F32),
                dma((4,)),
                dma((8,)),
                dma((planes,)),
                dma((planes,)),
                dma((planes, frames, 2)),
                dma,
                dma,
                dma((1 + halves * (planes - 1),)),
                dma((1 + halves * (planes - 1),)),
                dma((planes * halves,)),
                dma((planes * halves,)),
                dma((planes,)),
                dma((planes,)),
                dma,
                dma,
            ],
            compiler_params=pltpu.CompilerParams(
                collective_id=0, has_side_effects=True, vmem_limit_bytes=56 * 1024 * 1024
            ),
        )(
            baseline,
            ktrans,
            plasma_volume,
            arterial,
            arterial_integral,
            sensitivity[0],
            kdata[0, 0],
            sampling[0],
            *[jnp.asarray(tab) for tab in tabs],
        )
        return tuple(sum(out[n, f] for f in range(frames)) for n in range(2))

    in_specs = (
        P("frame", "coil", None, None, "pencil", None),
        P("frame", None, None),
        P("coil", None, "pencil", None, None),
        P(None, "pencil", ("coil", "frame"), None),
        P("pencil", ("coil", "frame"), None),
        P("pencil", ("coil", "frame"), None),
        P("frame"),
        P("frame"),
    )
    out_specs = (P("pencil", ("coil", "frame"), None), P("pencil", ("coil", "frame"), None))
    return jax.shard_map(
        per_device, mesh=mesh, in_specs=in_specs, out_specs=out_specs, check_vma=False
    )
```

```python
import math

import jax
import jax.numpy as jnp
import numpy as np
from jax import lax
from jax.experimental import pallas as pl
from jax.experimental.pallas import tpu as pltpu
from jax.sharding import PartitionSpec as P

MESH = pl.DeviceIdType.MESH
F32 = jnp.float32
BF16 = jnp.bfloat16


def tables(size):
    index = np.arange(size)
    product = index[:, None] * index[None, :] % size
    angle = product.astype(np.float32) * np.float32(2.0 * math.pi / size)
    scale = np.float32(1.0 / math.sqrt(size))
    return (
        (np.cos(angle.astype(np.float64)).astype(np.float32) * scale).astype(BF16),
        (np.sin(angle.astype(np.float64)).astype(np.float32) * scale).astype(BF16),
    )


def complex_table(size):
    cos_t, sin_t = tables(size)
    return np.stack(
        [
            np.stack([cos_t.T, sin_t.T], axis=1),
            np.stack([-sin_t.T, cos_t.T], axis=1),
        ]
    )


def all_tables(nx, ny, nz, pencils):
    lines, planes = nx // pencils, nz // pencils
    cos_y, sin_y = tables(ny)
    rows_y = np.concatenate([cos_y, sin_y], axis=1)
    full_x = complex_table(nx)
    forward_x = (
        full_x.reshape(2, pencils, lines, 2 * nx)
        .transpose(1, 0, 2, 3)
        .reshape(2 * nx, 2 * nx)
    )
    inverse_x = np.ascontiguousarray(forward_x.T)
    full_z = complex_table(nz)
    spread = np.einsum(
        "akbz,ij->akibzj", full_z.astype(np.float32), np.eye(lines, dtype=np.float32)
    )
    spread = spread.reshape(2, nz, lines, 2, pencils, planes, lines)
    forward_z = (
        spread.transpose(5, 0, 1, 2, 4, 3, 6)
        .reshape(planes, 2 * nz * lines, pencils * 2 * lines)
        .astype(BF16)
    )
    inverse_z = np.ascontiguousarray(forward_z.transpose(0, 2, 1))
    return rows_y, forward_x, inverse_x, forward_z, inverse_z


def dot(a, b):
    return jnp.dot(a, b, preferred_element_type=F32)


def split(value):
    high = value.astype(BF16)
    return high, (value - high.astype(F32)).astype(BF16)


def far_first(n, size):
    return size // 2 + (1 - 2 * lax.rem(n, 2)) * ((n + 1) // 2)


def kernel(
    sizes,
    base_in,
    ktrans_in,
    volume_in,
    arterial,
    integral,
    sens_in,
    kdata_in,
    sampling_in,
    rows_y_in,
    forward_x_in,
    inverse_x_in,
    forward_z_in,
    inverse_z_in,
    out,
    own_base,
    own_params,
    own_frames,
    images,
    bases,
    sens,
    kdata,
    sampling,
    rows_y,
    forward_x,
    inverse_x,
    forward_z,
    inverse_z,
    send_f,
    recv_f,
    kspace,
    residual,
    send_b,
    recv_b,
    send_p,
    recv_p,
    weights,
    own_sem,
    load_sem,
    isend_sem,
    irecv_sem,
    relay_sem,
    base_send,
    base_recv,
    fsend_sem,
    frecv_sem,
    bsend_sem,
    brecv_sem,
    psend_sem,
    precv_sem,
    wsend_sem,
    wrecv_sem,
):
    coils, pencils, frames = sizes
    planes, owners = images.shape[:2]
    nx, ny = sens.shape[2:]
    halves, width = send_f.shape[1], send_f.shape[-1]
    c = lax.axis_index("coil")
    p = lax.axis_index("pencil")
    t = lax.axis_index("frame")
    me = c * frames + t
    other = 1 - t

    own = [
        pltpu.make_async_copy(base_in.at[0], own_base.at[:, 0], own_sem.at[0]),
        pltpu.make_async_copy(base_in.at[1], own_base.at[:, 1], own_sem.at[1]),
        pltpu.make_async_copy(ktrans_in, own_params.at[0], own_sem.at[2]),
        pltpu.make_async_copy(volume_in, own_params.at[1], own_sem.at[3]),
    ]
    for copy in own:
        copy.start()
    barrier = pltpu.get_barrier_semaphore()

    def greet_pencil(d, carry):
        peer = lax.rem(p + d, pencils)
        pl.semaphore_signal(barrier, inc=1, device_id={"pencil": peer}, device_id_type=MESH)
        return carry

    lax.fori_loop(1, pencils, greet_pencil, 0)

    def greet_maps(d, carry):
        peer = lax.rem(me + d, coils * frames)
        pl.semaphore_signal(
            barrier,
            inc=1,
            device_id={"coil": peer // frames, "frame": lax.rem(peer, frames)},
            device_id_type=MESH,
        )
        return carry

    lax.fori_loop(1, coils * frames, greet_maps, 0)

    pairs = [
        (rows_y_in, rows_y),
        (sens_in, sens),
        (forward_x_in, forward_x),
        (forward_z_in, forward_z),
        (kdata_in, kdata),
        (sampling_in, sampling),
        (inverse_z_in, inverse_z),
        (inverse_x_in, inverse_x),
    ]
    loads = [
        pltpu.make_async_copy(src, dst, load_sem.at[n])
        for n, (src, dst) in enumerate(pairs)
    ]
    for copy in loads:
        copy.start()

    weights[t, 0] = jnp.full(weights.shape[2:], integral[0], F32)
    weights[t, 1] = jnp.full(weights.shape[2:], arterial[0], F32)

    def frame_rows(frame):
        factor = (
            1.0
            + weights[frame, 0] * own_params[0].astype(F32)
            + weights[frame, 1] * own_params[1].astype(F32)
        )
        own_frames[frame] = (own_base[...].astype(F32) * factor[:, None]).astype(BF16)

    for copy in own:
        copy.wait()
    frame_rows(t)
    pl.semaphore_wait(barrier, pencils - 1 + owners - 1)
    weight_copy = pltpu.make_async_remote_copy(
        weights.at[t],
        weights.at[t],
        wsend_sem,
        wrecv_sem,
        device_id={"frame": other},
        device_id_type=MESH,
    )
    weight_copy.start()

    near = 4

    def far_pencil(n):
        ring = lax.rem(p // near + far_first(n // near, pencils // near), pencils // near)
        return ring * near + lax.rem(lax.rem(p, near) + lax.rem(n + 1, near), near)

    def far_owner(n):
        coil = lax.rem(c + far_first(n // frames, coils), coils)
        return coil, lax.rem(t + lax.rem(n + 1, frames), frames)

    def images_direct(frame, count):
        def one(n, carry):
            pltpu.make_async_remote_copy(
                own_frames.at[frame, 0],
                images.at[0, me],
                isend_sem.at[0],
                irecv_sem.at[0],
                device_id={"coil": lax.rem(c + far_first(n, coils), coils), "frame": frame},
                device_id_type=MESH,
            ).start()
            return carry

        lax.fori_loop(0, count, one, 0)

    def image_copy(block, i, sem, coil, frame):
        pltpu.make_async_remote_copy(
            block,
            images.at[i, me] if frame is not None else block,
            isend_sem.at[i],
            sem,
            device_id={"coil": lax.rem(coil + coils, coils)}
            | ({} if frame is None else {"frame": frame}),
            device_id_type=MESH,
        ).start()

    def images_to(i, frame):
        block = own_frames.at[frame, i]
        image_copy(block, i, relay_sem.at[i, t, 0], c + 2, frame)
        image_copy(block, i, relay_sem.at[i, t, 1], c - 2, frame)
        image_copy(block, i, irecv_sem.at[i], c + 1, frame)
        image_copy(block, i, irecv_sem.at[i], c - 1, frame)
        if frame is other:
            image_copy(block, i, irecv_sem.at[i], c, frame)

    def relay(i):
        for way, step in ((0, 1), (1, -1)):
            for frame in (t, other):
                block = images.at[
                    i, lax.rem(c - 2 * step + coils, coils) * frames + frame
                ]
                pltpu.make_async_copy(block, block, relay_sem.at[i, frame, way]).wait()
                image_copy(block, i, irecv_sem.at[i], c + step, None)
                if (way == 0) == (frame is t):
                    image_copy(block, i, irecv_sem.at[i], c + 2 * step, None)

    def bases_to(d, carry):
        peer = lax.rem(me + d, owners)
        pltpu.make_async_remote_copy(
            own_base,
            bases.at[me],
            base_send,
            base_recv,
            device_id={"coil": peer // frames, "frame": lax.rem(peer, frames)},
            device_id_type=MESH,
        ).start()
        return carry

    slabs = [(h, i) for h in range(halves) for i in range(1, planes)]
    parts = [(slice(None), 0), *slabs]

    def send_forward(n):
        exchange(send_f, recv_f, fsend_sem, frecv_sem, n, parts[n])

    def forward(i):
        shape = (nx, images.shape[-1])
        frame_re = images[i, :, 0].reshape(shape).astype(F32)
        frame_im = images[i, :, 1].reshape(shape).astype(F32)
        sens_re = sens[0, i].astype(F32)
        sens_im = sens[1, i].astype(F32)
        high, low = split(
            jnp.concatenate(
                [
                    sens_re * frame_re - sens_im * frame_im,
                    sens_re * frame_im + sens_im * frame_re,
                ],
                axis=0,
            )
        )
        y = dot(high, rows_y[...]) + dot(low, rows_y[...])
        high, low = split(
            jnp.concatenate(
                [y[:nx, :ny] + y[nx:, ny:], y[nx:, :ny] - y[:nx, ny:]], axis=0
            )
        )
        x = dot(forward_x[...], high) + dot(forward_x[...], low)
        for h in range(halves):
            cut = x[:, h * width : (h + 1) * width]
            send_f[:, h, i] = cut.astype(BF16).reshape(pencils, -1, width)
        recv_f[p, :, i] = send_f[p, :, i]
        if i == 0:
            send_forward(0)
        else:
            send_forward(1 + slabs.index((0, i)))
        if i == planes - 1:
            for n in range(planes, len(slabs) + 1):
                send_forward(n)

    def exchange(src, dst, send_sem, recv_sem, n, part):
        def one(n_peer, carry):
            peer = far_pencil(n_peer)
            pltpu.make_async_remote_copy(
                src.at[(peer, *part)],
                dst.at[(p, *part)],
                send_sem.at[n],
                recv_sem.at[n],
                device_id={"pencil": peer},
                device_id_type=MESH,
            ).start()
            return carry

        lax.fori_loop(0, pencils - 1, one, 0)

    def all_but_one(ref, part, sem):
        view = ref.at[(pl.ds(0, pencils - 1), *part)]
        pltpu.make_async_copy(view, view, sem).wait()

    def wait_bytes(ref, i, count, sem):
        view = ref.at[i, pl.ds(0, count)]
        pltpu.make_async_copy(view, view, sem.at[i]).wait()

    images_direct(t, coils - 1)
    weight_copy.wait()
    frame_rows(other)
    images_direct(other, coils)
    for i in range(1, planes):
        images_to(i, t)
        images_to(i, other)
    images[:, me] = own_frames[t]
    bases[me] = own_base[...]
    for copy in loads[:3]:
        copy.wait()
    for i in range(planes):
        wait_bytes(images, i, owners - (1 if i == 0 else 5), irecv_sem)
        forward(i)
        if i == 0:
            for later in range(1, planes):
                relay(later)
    lax.fori_loop(1, owners, bases_to, 0)

    for copy in loads[3:6]:
        copy.wait()
    all_but_one(recv_f, parts[0], frecv_sem.at[0])
    lines = jnp.concatenate(
        [recv_f[:, h, 0].reshape(-1, width) for h in range(halves)], axis=1
    )
    kspace[...] = dot(forward_z[0], lines) - kdata[...].astype(F32).reshape(kspace.shape)
    loads[6].wait()
    half_rows = kspace.shape[0] // 2
    for h in range(halves):
        columns = slice(h * width, (h + 1) * width)
        for i in range(1, planes):
            all_but_one(recv_f, (h, i), frecv_sem.at[1 + slabs.index((h, i))])
            lines = recv_f[:, h, i].reshape(-1, width)
            if i < planes - 1:
                kspace[:, columns] = dot(forward_z[i], lines) + kspace[:, columns]
        keep = sampling[:, columns].astype(F32)[:, None, :]
        for part in range(2):
            rows = slice(part * half_rows, (part + 1) * half_rows)
            value = dot(forward_z[planes - 1, rows, :], lines) + kspace[rows, columns]
            value = keep * value.reshape(keep.shape[0], -1, width)
            high, low = split(value.reshape(half_rows, width))
            residual[h, rows, :width] = high
            residual[h, rows, width:] = low
        for i in range(planes):
            x = dot(inverse_z[i], residual[h])
            x = (x[:, :width] + x[:, width:]).astype(BF16)
            send_b[:, h, i] = x.reshape(pencils, -1, width)
            recv_b[p, h, i] = send_b[p, h, i]
            exchange(send_b, recv_b, bsend_sem, brecv_sem, h * planes + i, (h, i))

    loads[7].wait()
    base_blocks = bases.at[pl.ds(0, owners - 1)]
    pltpu.make_async_copy(base_blocks, base_blocks, base_recv).wait()
    for i in range(planes):
        for h in range(halves):
            all_but_one(recv_b, (h, i), brecv_sem.at[h * planes + i])
        lines = jnp.concatenate(
            [recv_b[:, h, i].reshape(-1, width) for h in range(halves)], axis=1
        )
        x = dot(inverse_x[...], lines)
        high, low = split(x)
        y = dot(high, rows_y[...]) + dot(low, rows_y[...])
        back_re = y[:nx, :ny] - y[nx:, ny:]
        back_im = y[nx:, :ny] + y[:nx, ny:]
        sens_re = sens[0, i].astype(F32)
        sens_im = sens[1, i].astype(F32)
        adj_re = sens_re * back_re + sens_im * back_im
        adj_im = sens_re * back_im - sens_im * back_re
        base_re = bases[:, i, 0].reshape(nx, ny).astype(F32)
        base_im = bases[:, i, 1].reshape(nx, ny).astype(F32)
        terms = base_re * adj_re + base_im * adj_im
        send_p[i] = terms.astype(BF16).reshape(send_p.shape[1:])
        recv_p[i, me] = send_p[i, me]

        def hand(n, carry):
            coil, frame = far_owner(n)
            pltpu.make_async_remote_copy(
                send_p.at[i, coil * frames + frame],
                recv_p.at[i, me],
                psend_sem.at[i],
                precv_sem.at[i],
                device_id={"coil": coil, "frame": frame},
                device_id_type=MESH,
            ).start()
            return carry

        lax.fori_loop(0, owners - 1, hand, 0)

    for i in range(planes):
        wait_bytes(recv_p, i, owners - 1, precv_sem)
        for f in range(frames):
            total = sum(recv_p[i, n * frames + f].astype(F32) for n in range(coils))
            for n in range(2):
                out[n, f, i] = weights[f, n] * total

    for i in range(planes):
        wait_bytes(images, i, owners - 1, isend_sem)
        for h in range(halves):
            all_but_one(send_b, (h, i), bsend_sem.at[h * planes + i])
        wait_bytes(send_p, i, owners - 1, psend_sem)
    for n, part in enumerate(parts):
        all_but_one(send_f, part, fsend_sem.at[n])
    pltpu.make_async_copy(base_blocks, base_blocks, base_send).wait()


def solution(mesh):
    coils, pencils, frames = mesh.shape["coil"], mesh.shape["pencil"], mesh.shape["frame"]

    def per_device(
        kdata, sampling, sensitivity, baseline, ktrans, plasma_volume, arterial, arterial_integral
    ):
        planes, rows, ny = ktrans.shape
        nx = sensitivity.shape[3]
        nz = kdata.shape[3]
        lines = kdata.shape[4]
        owners = coils * frames
        tabs = all_tables(nx, ny, nz, pencils)
        hbm = pl.BlockSpec(memory_space=pltpu.HBM)
        smem = pl.BlockSpec(memory_space=pltpu.SMEM)
        vmem = pl.BlockSpec(memory_space=pltpu.VMEM)
        dma = pltpu.SemaphoreType.DMA
        halves = 2 if ny % 256 == 0 else 1
        blocks = (pencils, halves, planes, 2 * lines, ny // halves)
        out = pl.pallas_call(
            lambda *refs: kernel((coils, pencils, frames), *refs),
            out_shape=jax.ShapeDtypeStruct((2, frames, planes, rows, ny), F32),
            in_specs=[hbm, hbm, hbm, smem, smem] + [hbm] * 8,
            out_specs=vmem,
            scratch_shapes=[
                pltpu.VMEM((planes, 2, rows, ny), BF16),
                pltpu.VMEM((2, planes, rows, ny), BF16),
                pltpu.VMEM((frames, planes, 2, rows, ny), BF16),
                pltpu.VMEM((planes, owners, 2, rows, ny), BF16),
                pltpu.VMEM((owners, planes, 2, rows, ny), BF16),
                pltpu.VMEM((2, planes, nx, ny), BF16),
                pltpu.VMEM((2, nz, lines, ny), BF16),
                pltpu.VMEM((nz, ny), jnp.int32),
                *[pltpu.VMEM(tab.shape, BF16) for tab in tabs],
                pltpu.VMEM(blocks, BF16),
                pltpu.VMEM(blocks, BF16),
                pltpu.VMEM((2 * nz * lines, ny), F32),
                pltpu.VMEM((halves, 2 * nz * lines, 2 * ny // halves), BF16),
                pltpu.VMEM(blocks, BF16),
                pltpu.VMEM(blocks, BF16),
                pltpu.VMEM((planes, owners, rows, ny), BF16),
                pltpu.VMEM((planes, owners, rows, ny), BF16),
                pltpu.VMEM((frames, 2, rows, ny), F32),
                dma((4,)),
                dma((8,)),
                dma((planes,)),
                dma((planes,)),
                dma((planes, frames, 2)),
                dma,
                dma,
                dma((1 + halves * (planes - 1),)),
                dma((1 + halves * (planes - 1),)),
                dma((planes * halves,)),
                dma((planes * halves,)),
                dma((planes,)),
                dma((planes,)),
                dma,
                dma,
            ],
            compiler_params=pltpu.CompilerParams(
                collective_id=0, has_side_effects=True, vmem_limit_bytes=56 * 1024 * 1024
            ),
        )(
            baseline,
            ktrans,
            plasma_volume,
            arterial,
            arterial_integral,
            sensitivity[0],
            kdata[0, 0],
            sampling[0],
            *[jnp.asarray(tab) for tab in tabs],
        )
        return tuple(sum(out[n, f] for f in range(frames)) for n in range(2))

    in_specs = (
        P("frame", "coil", None, None, "pencil", None),
        P("frame", None, None),
        P("coil", None, "pencil", None, None),
        P(None, "pencil", ("coil", "frame"), None),
        P("pencil", ("coil", "frame"), None),
        P("pencil", ("coil", "frame"), None),
        P("frame"),
        P("frame"),
    )
    out_specs = (P("pencil", ("coil", "frame"), None), P("pencil", ("coil", "frame"), None))
    return jax.shard_map(
        per_device, mesh=mesh, in_specs=in_specs, out_specs=out_specs, check_vma=False
    )
```

```python
import math

import jax
import jax.numpy as jnp
import numpy as np
from jax import lax
from jax.experimental import pallas as pl
from jax.experimental.pallas import tpu as pltpu
from jax.sharding import PartitionSpec as P

MESH = pl.DeviceIdType.MESH
F32 = jnp.float32
BF16 = jnp.bfloat16


def tables(size):
    index = np.arange(size)
    product = index[:, None] * index[None, :] % size
    angle = product.astype(np.float32) * np.float32(2.0 * math.pi / size)
    scale = np.float32(1.0 / math.sqrt(size))
    return (
        (np.cos(angle.astype(np.float64)).astype(np.float32) * scale).astype(BF16),
        (np.sin(angle.astype(np.float64)).astype(np.float32) * scale).astype(BF16),
    )


def complex_table(size):
    cos_t, sin_t = tables(size)
    return np.stack(
        [
            np.stack([cos_t.T, sin_t.T], axis=1),
            np.stack([-sin_t.T, cos_t.T], axis=1),
        ]
    )


def all_tables(nx, ny, nz, pencils):
    lines, planes = nx // pencils, nz // pencils
    cos_y, sin_y = tables(ny)
    rows_y = np.concatenate([cos_y, sin_y], axis=1)
    full_x = complex_table(nx)
    forward_x = (
        full_x.reshape(2, pencils, lines, 2 * nx)
        .transpose(1, 0, 2, 3)
        .reshape(2 * nx, 2 * nx)
    )
    inverse_x = np.ascontiguousarray(forward_x.T)
    full_z = complex_table(nz)
    spread = np.einsum(
        "akbz,ij->akibzj", full_z.astype(np.float32), np.eye(lines, dtype=np.float32)
    )
    spread = spread.reshape(2, nz, lines, 2, pencils, planes, lines)
    forward_z = (
        spread.transpose(5, 0, 1, 2, 4, 3, 6)
        .reshape(planes, 2 * nz * lines, pencils * 2 * lines)
        .astype(BF16)
    )
    inverse_z = np.ascontiguousarray(forward_z.transpose(0, 2, 1))
    return rows_y, forward_x, inverse_x, forward_z, inverse_z


def dot(a, b):
    return jnp.dot(a, b, preferred_element_type=F32)


def split(value):
    high = value.astype(BF16)
    return high, (value - high.astype(F32)).astype(BF16)


def far_first(n, size):
    return size // 2 + (1 - 2 * lax.rem(n, 2)) * ((n + 1) // 2)


def kernel(
    sizes,
    base_in,
    ktrans_in,
    volume_in,
    arterial,
    integral,
    sens_in,
    kdata_in,
    sampling_in,
    rows_y_in,
    forward_x_in,
    inverse_x_in,
    forward_z_in,
    inverse_z_in,
    out,
    own_base,
    own_params,
    own_frames,
    images,
    bases,
    sens,
    kdata,
    sampling,
    rows_y,
    forward_x,
    inverse_x,
    forward_z,
    inverse_z,
    send_f,
    recv_f,
    kspace,
    residual,
    send_b,
    recv_b,
    send_p,
    recv_p,
    weights,
    own_sem,
    load_sem,
    isend_sem,
    irecv_sem,
    relay_sem,
    base_send,
    base_recv,
    base_cross,
    fsend_sem,
    frecv_sem,
    bsend_sem,
    brecv_sem,
    psend_sem,
    precv_sem,
    wsend_sem,
    wrecv_sem,
):
    coils, pencils, frames = sizes
    planes, owners = images.shape[:2]
    nx, ny = sens.shape[2:]
    halves, width = send_f.shape[1], send_f.shape[-1]
    c = lax.axis_index("coil")
    p = lax.axis_index("pencil")
    t = lax.axis_index("frame")
    me = c * frames + t
    other = 1 - t

    own = [
        pltpu.make_async_copy(base_in.at[0], own_base.at[:, 0], own_sem.at[0]),
        pltpu.make_async_copy(base_in.at[1], own_base.at[:, 1], own_sem.at[1]),
        pltpu.make_async_copy(ktrans_in, own_params.at[0], own_sem.at[2]),
        pltpu.make_async_copy(volume_in, own_params.at[1], own_sem.at[3]),
    ]
    for copy in own:
        copy.start()
    near = 4

    def far_pencil(n):
        ring = lax.rem(p // near + far_first(n // near, pencils // near), pencils // near)
        return ring * near + lax.rem(lax.rem(p, near) + lax.rem(n + 1, near), near)

    def far_owner(n):
        coil = lax.rem(c + far_first(n // frames, coils), coils)
        return coil, lax.rem(t + lax.rem(n + 1, frames), frames)

    barrier = pltpu.get_barrier_semaphore()

    def greet_owner(n, carry):
        coil, frame = far_owner(n)
        pl.semaphore_signal(
            barrier, inc=1, device_id={"coil": coil, "frame": frame}, device_id_type=MESH
        )
        return carry

    def greet_pencil(n, carry):
        pl.semaphore_signal(
            barrier, inc=1, device_id={"pencil": far_pencil(n)}, device_id_type=MESH
        )
        return carry

    lax.fori_loop(0, owners - 1, greet_owner, 0)
    lax.fori_loop(0, pencils - 1, greet_pencil, 0)

    pairs = [
        (rows_y_in, rows_y),
        (sens_in, sens),
        (forward_x_in, forward_x),
        (forward_z_in, forward_z),
        (kdata_in, kdata),
        (sampling_in, sampling),
        (inverse_z_in, inverse_z),
        (inverse_x_in, inverse_x),
    ]
    loads = [
        pltpu.make_async_copy(src, dst, load_sem.at[n])
        for n, (src, dst) in enumerate(pairs)
    ]
    for copy in loads:
        copy.start()

    weights[t, 0] = jnp.full(weights.shape[2:], integral[0], F32)
    weights[t, 1] = jnp.full(weights.shape[2:], arterial[0], F32)

    def frame_rows(frame):
        factor = (
            1.0
            + weights[frame, 0] * own_params[0].astype(F32)
            + weights[frame, 1] * own_params[1].astype(F32)
        )
        own_frames[frame] = (own_base[...].astype(F32) * factor[:, None]).astype(BF16)

    for copy in own:
        copy.wait()
    frame_rows(t)
    pl.semaphore_wait(barrier, pencils - 1 + owners - 1)
    weight_copy = pltpu.make_async_remote_copy(
        weights.at[t],
        weights.at[t],
        wsend_sem,
        wrecv_sem,
        device_id={"frame": other},
        device_id_type=MESH,
    )
    weight_copy.start()

    def images_direct(frame, count):
        def one(n, carry):
            pltpu.make_async_remote_copy(
                own_frames.at[frame, 0],
                images.at[0, me],
                isend_sem.at[0],
                irecv_sem.at[0],
                device_id={"coil": lax.rem(c + far_first(n, coils), coils), "frame": frame},
                device_id_type=MESH,
            ).start()
            return carry

        lax.fori_loop(0, count, one, 0)

    def image_copy(block, i, sem, coil, frame):
        pltpu.make_async_remote_copy(
            block,
            images.at[i, me] if frame is not None else block,
            isend_sem.at[i],
            sem,
            device_id={"coil": lax.rem(coil + coils, coils)}
            | ({} if frame is None else {"frame": frame}),
            device_id_type=MESH,
        ).start()

    def images_to(i, frame):
        block = own_frames.at[frame, i]
        image_copy(block, i, relay_sem.at[i, t, 0], c + 2, frame)
        image_copy(block, i, relay_sem.at[i, t, 1], c - 2, frame)
        image_copy(block, i, irecv_sem.at[i], c + 1, frame)
        image_copy(block, i, irecv_sem.at[i], c - 1, frame)
        if frame is other:
            image_copy(block, i, irecv_sem.at[i], c, frame)

    def relay(i):
        for way, step in ((0, 1), (1, -1)):
            for frame in (t, other):
                block = images.at[
                    i, lax.rem(c - 2 * step + coils, coils) * frames + frame
                ]
                pltpu.make_async_copy(block, block, relay_sem.at[i, frame, way]).wait()
                image_copy(block, i, irecv_sem.at[i], c + step, None)
                if (way == 0) == (frame is t):
                    image_copy(block, i, irecv_sem.at[i], c + 2 * step, None)

    def base_copy(owner, sem, device):
        block = bases.at[owner]
        pltpu.make_async_remote_copy(
            block, block, base_send, sem, device_id=device, device_id_type=MESH
        ).start()

    def bases_along(owner):
        def one(n, carry):
            base_copy(owner, base_recv, {"coil": lax.rem(c + far_first(n, coils), coils)})
            return carry

        lax.fori_loop(0, coils - 1, one, 0)

    slabs = [(h, i) for h in range(halves) for i in range(1, planes)]
    parts = [(slice(None), 0), *slabs]

    def send_forward(n):
        exchange(send_f, recv_f, fsend_sem, frecv_sem, n, parts[n])

    def forward(i):
        shape = (nx, images.shape[-1])
        frame_re = images[i, :, 0].reshape(shape).astype(F32)
        frame_im = images[i, :, 1].reshape(shape).astype(F32)
        sens_re = sens[0, i].astype(F32)
        sens_im = sens[1, i].astype(F32)
        high, low = split(
            jnp.concatenate(
                [
                    sens_re * frame_re - sens_im * frame_im,
                    sens_re * frame_im + sens_im * frame_re,
                ],
                axis=0,
            )
        )
        y = dot(high, rows_y[...]) + dot(low, rows_y[...])
        high, low = split(
            jnp.concatenate(
                [y[:nx, :ny] + y[nx:, ny:], y[nx:, :ny] - y[:nx, ny:]], axis=0
            )
        )
        x = dot(forward_x[...], high) + dot(forward_x[...], low)
        for h in range(halves):
            cut = x[:, h * width : (h + 1) * width]
            send_f[:, h, i] = cut.astype(BF16).reshape(pencils, -1, width)
        recv_f[p, :, i] = send_f[p, :, i]
        if i == 0:
            send_forward(0)
        else:
            send_forward(1 + slabs.index((0, i)))
        if i == planes - 1:
            for n in range(planes, len(slabs) + 1):
                send_forward(n)

    def exchange(src, dst, send_sem, recv_sem, n, part):
        def one(n_peer, carry):
            peer = far_pencil(n_peer)
            pltpu.make_async_remote_copy(
                src.at[(peer, *part)],
                dst.at[(p, *part)],
                send_sem.at[n],
                recv_sem.at[n],
                device_id={"pencil": peer},
                device_id_type=MESH,
            ).start()
            return carry

        lax.fori_loop(0, pencils - 1, one, 0)

    def all_but_one(ref, part, sem):
        view = ref.at[(pl.ds(0, pencils - 1), *part)]
        pltpu.make_async_copy(view, view, sem).wait()

    def wait_bytes(ref, i, count, sem):
        view = ref.at[i, pl.ds(0, count)]
        pltpu.make_async_copy(view, view, sem.at[i]).wait()

    images_direct(t, coils - 1)
    weight_copy.wait()
    frame_rows(other)
    images_direct(other, coils)
    for i in range(1, planes):
        images_to(i, t)
        images_to(i, other)
    images[:, me] = own_frames[t]
    bases[me] = own_base[...]
    for copy in loads[:3]:
        copy.wait()
    for i in range(planes):
        wait_bytes(images, i, owners - (1 if i == 0 else 5), irecv_sem)
        forward(i)
        if i == 0:
            for later in range(1, planes):
                relay(later)
    base_copy(me, base_cross, {"frame": other})
    bases_along(me)

    for copy in loads[3:6]:
        copy.wait()
    all_but_one(recv_f, parts[0], frecv_sem.at[0])
    partner = c * frames + other
    crossed = bases.at[partner]
    pltpu.make_async_copy(crossed, crossed, base_cross).wait()
    bases_along(partner)
    lines = jnp.concatenate(
        [recv_f[:, h, 0].reshape(-1, width) for h in range(halves)], axis=1
    )
    kspace[...] = dot(forward_z[0], lines) - kdata[...].astype(F32).reshape(kspace.shape)
    loads[6].wait()
    half_rows = kspace.shape[0] // 2
    for h in range(halves):
        columns = slice(h * width, (h + 1) * width)
        for i in range(1, planes):
            all_but_one(recv_f, (h, i), frecv_sem.at[1 + slabs.index((h, i))])
            lines = recv_f[:, h, i].reshape(-1, width)
            if i < planes - 1:
                kspace[:, columns] = dot(forward_z[i], lines) + kspace[:, columns]
        keep = sampling[:, columns].astype(F32)[:, None, :]
        for part in range(2):
            rows = slice(part * half_rows, (part + 1) * half_rows)
            value = dot(forward_z[planes - 1, rows, :], lines) + kspace[rows, columns]
            value = keep * value.reshape(keep.shape[0], -1, width)
            high, low = split(value.reshape(half_rows, width))
            residual[h, rows, :width] = high
            residual[h, rows, width:] = low
        for i in range(planes):
            x = dot(inverse_z[i], residual[h])
            x = (x[:, :width] + x[:, width:]).astype(BF16)
            send_b[:, h, i] = x.reshape(pencils, -1, width)
            recv_b[p, h, i] = send_b[p, h, i]
            exchange(send_b, recv_b, bsend_sem, brecv_sem, h * planes + i, (h, i))

    loads[7].wait()
    base_blocks = bases.at[pl.ds(0, owners - 1)]
    along_blocks = bases.at[pl.ds(0, owners - frames)]
    pltpu.make_async_copy(along_blocks, along_blocks, base_recv).wait()
    for i in range(planes):
        for h in range(halves):
            all_but_one(recv_b, (h, i), brecv_sem.at[h * planes + i])
        lines = jnp.concatenate(
            [recv_b[:, h, i].reshape(-1, width) for h in range(halves)], axis=1
        )
        x = dot(inverse_x[...], lines)
        high, low = split(x)
        y = dot(high, rows_y[...]) + dot(low, rows_y[...])
        back_re = y[:nx, :ny] - y[nx:, ny:]
        back_im = y[nx:, :ny] + y[:nx, ny:]
        sens_re = sens[0, i].astype(F32)
        sens_im = sens[1, i].astype(F32)
        adj_re = sens_re * back_re + sens_im * back_im
        adj_im = sens_re * back_im - sens_im * back_re
        base_re = bases[:, i, 0].reshape(nx, ny).astype(F32)
        base_im = bases[:, i, 1].reshape(nx, ny).astype(F32)
        terms = base_re * adj_re + base_im * adj_im
        send_p[i] = terms.astype(BF16).reshape(send_p.shape[1:])
        recv_p[i, me] = send_p[i, me]

        def hand(n, carry):
            coil, frame = far_owner(n)
            pltpu.make_async_remote_copy(
                send_p.at[i, coil * frames + frame],
                recv_p.at[i, me],
                psend_sem.at[i],
                precv_sem.at[i],
                device_id={"coil": coil, "frame": frame},
                device_id_type=MESH,
            ).start()
            return carry

        lax.fori_loop(0, owners - 1, hand, 0)

    for i in range(planes):
        wait_bytes(recv_p, i, owners - 1, precv_sem)
        for f in range(frames):
            total = sum(recv_p[i, n * frames + f].astype(F32) for n in range(coils))
            for n in range(2):
                out[n, f, i] = weights[f, n] * total

    for i in range(planes):
        wait_bytes(images, i, owners - 1, isend_sem)
        for h in range(halves):
            all_but_one(send_b, (h, i), bsend_sem.at[h * planes + i])
        wait_bytes(send_p, i, owners - 1, psend_sem)
    for n, part in enumerate(parts):
        all_but_one(send_f, part, fsend_sem.at[n])
    pltpu.make_async_copy(base_blocks, base_blocks, base_send).wait()


def solution(mesh):
    coils, pencils, frames = mesh.shape["coil"], mesh.shape["pencil"], mesh.shape["frame"]

    def per_device(
        kdata, sampling, sensitivity, baseline, ktrans, plasma_volume, arterial, arterial_integral
    ):
        planes, rows, ny = ktrans.shape
        nx = sensitivity.shape[3]
        nz = kdata.shape[3]
        lines = kdata.shape[4]
        owners = coils * frames
        tabs = all_tables(nx, ny, nz, pencils)
        hbm = pl.BlockSpec(memory_space=pltpu.HBM)
        smem = pl.BlockSpec(memory_space=pltpu.SMEM)
        vmem = pl.BlockSpec(memory_space=pltpu.VMEM)
        dma = pltpu.SemaphoreType.DMA
        halves = 2 if ny % 256 == 0 else 1
        blocks = (pencils, halves, planes, 2 * lines, ny // halves)
        out = pl.pallas_call(
            lambda *refs: kernel((coils, pencils, frames), *refs),
            out_shape=jax.ShapeDtypeStruct((2, frames, planes, rows, ny), F32),
            in_specs=[hbm, hbm, hbm, smem, smem] + [hbm] * 8,
            out_specs=vmem,
            scratch_shapes=[
                pltpu.VMEM((planes, 2, rows, ny), BF16),
                pltpu.VMEM((2, planes, rows, ny), BF16),
                pltpu.VMEM((frames, planes, 2, rows, ny), BF16),
                pltpu.VMEM((planes, owners, 2, rows, ny), BF16),
                pltpu.VMEM((owners, planes, 2, rows, ny), BF16),
                pltpu.VMEM((2, planes, nx, ny), BF16),
                pltpu.VMEM((2, nz, lines, ny), BF16),
                pltpu.VMEM((nz, ny), jnp.int32),
                *[pltpu.VMEM(tab.shape, BF16) for tab in tabs],
                pltpu.VMEM(blocks, BF16),
                pltpu.VMEM(blocks, BF16),
                pltpu.VMEM((2 * nz * lines, ny), F32),
                pltpu.VMEM((halves, 2 * nz * lines, 2 * ny // halves), BF16),
                pltpu.VMEM(blocks, BF16),
                pltpu.VMEM(blocks, BF16),
                pltpu.VMEM((planes, owners, rows, ny), BF16),
                pltpu.VMEM((planes, owners, rows, ny), BF16),
                pltpu.VMEM((frames, 2, rows, ny), F32),
                dma((4,)),
                dma((8,)),
                dma((planes,)),
                dma((planes,)),
                dma((planes, frames, 2)),
                dma,
                dma,
                dma,
                dma((1 + halves * (planes - 1),)),
                dma((1 + halves * (planes - 1),)),
                dma((planes * halves,)),
                dma((planes * halves,)),
                dma((planes,)),
                dma((planes,)),
                dma,
                dma,
            ],
            compiler_params=pltpu.CompilerParams(
                collective_id=0, has_side_effects=True, vmem_limit_bytes=56 * 1024 * 1024
            ),
        )(
            baseline,
            ktrans,
            plasma_volume,
            arterial,
            arterial_integral,
            sensitivity[0],
            kdata[0, 0],
            sampling[0],
            *[jnp.asarray(tab) for tab in tabs],
        )
        return tuple(sum(out[n, f] for f in range(frames)) for n in range(2))

    in_specs = (
        P("frame", "coil", None, None, "pencil", None),
        P("frame", None, None),
        P("coil", None, "pencil", None, None),
        P(None, "pencil", ("coil", "frame"), None),
        P("pencil", ("coil", "frame"), None),
        P("pencil", ("coil", "frame"), None),
        P("frame"),
        P("frame"),
    )
    out_specs = (P("pencil", ("coil", "frame"), None), P("pencil", ("coil", "frame"), None))
    return jax.shard_map(
        per_device, mesh=mesh, in_specs=in_specs, out_specs=out_specs, check_vma=False
    )
```

```python
import math

import jax
import jax.numpy as jnp
import numpy as np
from jax import lax
from jax.experimental import pallas as pl
from jax.experimental.pallas import tpu as pltpu
from jax.sharding import PartitionSpec as P

MESH = pl.DeviceIdType.MESH
F32 = jnp.float32
BF16 = jnp.bfloat16


def tables(size):
    index = np.arange(size)
    product = index[:, None] * index[None, :] % size
    angle = product.astype(np.float32) * np.float32(2.0 * math.pi / size)
    scale = np.float32(1.0 / math.sqrt(size))
    return (
        (np.cos(angle.astype(np.float64)).astype(np.float32) * scale).astype(BF16),
        (np.sin(angle.astype(np.float64)).astype(np.float32) * scale).astype(BF16),
    )


def complex_table(size):
    cos_t, sin_t = tables(size)
    return np.stack(
        [
            np.stack([cos_t.T, sin_t.T], axis=1),
            np.stack([-sin_t.T, cos_t.T], axis=1),
        ]
    )


def all_tables(nx, ny, nz, pencils):
    lines, planes = nx // pencils, nz // pencils
    cos_y, sin_y = tables(ny)
    rows_y = np.concatenate([cos_y, sin_y], axis=1)
    full_x = complex_table(nx)
    forward_x = (
        full_x.reshape(2, pencils, lines, 2 * nx)
        .transpose(1, 0, 2, 3)
        .reshape(2 * nx, 2 * nx)
    )
    inverse_x = np.ascontiguousarray(forward_x.T)
    full_z = complex_table(nz)
    spread = np.einsum(
        "akbz,ij->akibzj", full_z.astype(np.float32), np.eye(lines, dtype=np.float32)
    )
    spread = spread.reshape(2, nz, lines, 2, pencils, planes, lines)
    forward_z = (
        spread.transpose(5, 0, 1, 2, 4, 3, 6)
        .reshape(planes, 2 * nz * lines, pencils * 2 * lines)
        .astype(BF16)
    )
    inverse_z = np.ascontiguousarray(forward_z.transpose(0, 2, 1))
    return rows_y, forward_x, inverse_x, forward_z, inverse_z


def dot(a, b):
    return jnp.dot(a, b, preferred_element_type=F32)


def split(value):
    high = value.astype(BF16)
    return high, (value - high.astype(F32)).astype(BF16)


def far_first(n, size):
    return size // 2 + (1 - 2 * lax.rem(n, 2)) * ((n + 1) // 2)


def kernel(
    sizes,
    base_in,
    ktrans_in,
    volume_in,
    arterial,
    integral,
    sens_in,
    kdata_in,
    sampling_in,
    rows_y_in,
    forward_x_in,
    inverse_x_in,
    forward_z_in,
    inverse_z_in,
    out,
    own_base,
    own_params,
    own_frames,
    images,
    bases,
    sens,
    kdata,
    sampling,
    rows_y,
    forward_x,
    inverse_x,
    forward_z,
    inverse_z,
    send_f,
    recv_f,
    kspace,
    residual,
    send_b,
    recv_b,
    send_p,
    recv_p,
    weights,
    own_sem,
    load_sem,
    isend_sem,
    irecv_sem,
    relay_sem,
    base_send,
    base_recv,
    base_cross,
    fsend_sem,
    frecv_sem,
    bsend_sem,
    brecv_sem,
    psend_sem,
    precv_sem,
    wsend_sem,
    wrecv_sem,
):
    coils, pencils, frames = sizes
    planes, owners = images.shape[:2]
    nx, ny = sens.shape[2:]
    halves, width = send_f.shape[1], send_f.shape[-1]
    c = lax.axis_index("coil")
    p = lax.axis_index("pencil")
    t = lax.axis_index("frame")
    me = c * frames + t
    other = 1 - t

    own = [
        pltpu.make_async_copy(base_in.at[0], own_base.at[:, 0], own_sem.at[0]),
        pltpu.make_async_copy(base_in.at[1], own_base.at[:, 1], own_sem.at[1]),
        pltpu.make_async_copy(ktrans_in, own_params.at[0], own_sem.at[2]),
        pltpu.make_async_copy(volume_in, own_params.at[1], own_sem.at[3]),
    ]
    for copy in own:
        copy.start()
    near = 4

    def far_pencil(n):
        ring = lax.rem(p // near + far_first(n // near, pencils // near), pencils // near)
        return ring * near + lax.rem(lax.rem(p, near) + lax.rem(n + 1, near), near)

    def far_owner(n):
        coil = lax.rem(c + far_first(n // frames, coils), coils)
        return coil, lax.rem(t + lax.rem(n + 1, frames), frames)

    barrier = pltpu.get_barrier_semaphore()

    def greet_owner(n, carry):
        coil, frame = far_owner(n)
        pl.semaphore_signal(
            barrier, inc=1, device_id={"coil": coil, "frame": frame}, device_id_type=MESH
        )
        return carry

    def greet_pencil(n, carry):
        pl.semaphore_signal(
            barrier, inc=1, device_id={"pencil": far_pencil(n)}, device_id_type=MESH
        )
        return carry

    lax.fori_loop(0, owners - 1, greet_owner, 0)
    lax.fori_loop(0, pencils - 1, greet_pencil, 0)

    pairs = [
        (rows_y_in, rows_y),
        (sens_in, sens),
        (forward_x_in, forward_x),
        (forward_z_in, forward_z),
        (kdata_in, kdata),
        (sampling_in, sampling),
        (inverse_z_in, inverse_z),
        (inverse_x_in, inverse_x),
    ]
    loads = [
        pltpu.make_async_copy(src, dst, load_sem.at[n])
        for n, (src, dst) in enumerate(pairs)
    ]
    for copy in loads:
        copy.start()

    weights[t, 0] = jnp.full(weights.shape[2:], integral[0], F32)
    weights[t, 1] = jnp.full(weights.shape[2:], arterial[0], F32)

    def frame_rows(frame):
        factor = (
            1.0
            + weights[frame, 0] * own_params[0].astype(F32)
            + weights[frame, 1] * own_params[1].astype(F32)
        )
        own_frames[frame] = (own_base[...].astype(F32) * factor[:, None]).astype(BF16)

    for copy in own:
        copy.wait()
    frame_rows(t)
    pl.semaphore_wait(barrier, pencils - 1 + owners - 1)
    weight_copy = pltpu.make_async_remote_copy(
        weights.at[t],
        weights.at[t],
        wsend_sem,
        wrecv_sem,
        device_id={"frame": other},
        device_id_type=MESH,
    )
    weight_copy.start()

    def images_direct(frame, count):
        def one(n, carry):
            pltpu.make_async_remote_copy(
                own_frames.at[frame, 0],
                images.at[0, me],
                isend_sem.at[0],
                irecv_sem.at[0],
                device_id={"coil": lax.rem(c + far_first(n, coils), coils), "frame": frame},
                device_id_type=MESH,
            ).start()
            return carry

        lax.fori_loop(0, count, one, 0)

    def image_copy(block, i, sem, coil, frame):
        pltpu.make_async_remote_copy(
            block,
            images.at[i, me] if frame is not None else block,
            isend_sem.at[i],
            sem,
            device_id={"coil": lax.rem(coil + coils, coils)}
            | ({} if frame is None else {"frame": frame}),
            device_id_type=MESH,
        ).start()

    def images_to(i, frame):
        block = own_frames.at[frame, i]
        image_copy(block, i, relay_sem.at[i, t, 0], c + 2, frame)
        image_copy(block, i, relay_sem.at[i, t, 1], c - 2, frame)
        image_copy(block, i, irecv_sem.at[i], c + 1, frame)
        image_copy(block, i, irecv_sem.at[i], c - 1, frame)
        if frame is other:
            image_copy(block, i, irecv_sem.at[i], c, frame)

    def relay(i):
        for way, step in ((0, 1), (1, -1)):
            for frame in (t, other):
                block = images.at[
                    i, lax.rem(c - 2 * step + coils, coils) * frames + frame
                ]
                pltpu.make_async_copy(block, block, relay_sem.at[i, frame, way]).wait()
                image_copy(block, i, irecv_sem.at[i], c + step, None)
                if (way == 0) == (frame is t):
                    image_copy(block, i, irecv_sem.at[i], c + 2 * step, None)

    def base_copy(owner, sem, device):
        block = bases.at[owner]
        pltpu.make_async_remote_copy(
            block, block, base_send, sem, device_id=device, device_id_type=MESH
        ).start()

    def bases_along(owner):
        def one(n, carry):
            base_copy(owner, base_recv, {"coil": lax.rem(c + far_first(n, coils), coils)})
            return carry

        lax.fori_loop(0, coils - 1, one, 0)

    slabs = [(h, i) for h in range(halves) for i in range(1, planes)]
    parts = [(slice(None), 0), *slabs]

    def send_forward(n):
        exchange(send_f, recv_f, fsend_sem, frecv_sem, n, parts[n])

    def forward(i):
        shape = (nx, images.shape[-1])
        frame_re = images[i, :, 0].reshape(shape).astype(F32)
        frame_im = images[i, :, 1].reshape(shape).astype(F32)
        sens_re = sens[0, i].astype(F32)
        sens_im = sens[1, i].astype(F32)
        high, low = split(
            jnp.concatenate(
                [
                    sens_re * frame_re - sens_im * frame_im,
                    sens_re * frame_im + sens_im * frame_re,
                ],
                axis=0,
            )
        )
        y = dot(high, rows_y[...]) + dot(low, rows_y[...])
        high, low = split(
            jnp.concatenate(
                [y[:nx, :ny] + y[nx:, ny:], y[nx:, :ny] - y[:nx, ny:]], axis=0
            )
        )
        x = dot(forward_x[...], high) + dot(forward_x[...], low)
        for h in range(halves):
            cut = x[:, h * width : (h + 1) * width]
            send_f[:, h, i] = cut.astype(BF16).reshape(pencils, -1, width)
        recv_f[p, :, i] = send_f[p, :, i]
        if i == 0:
            send_forward(0)
        else:
            send_forward(1 + slabs.index((0, i)))
        if i == planes - 1:
            for n in range(planes, len(slabs) + 1):
                send_forward(n)

    def exchange(src, dst, send_sem, recv_sem, n, part):
        def one(n_peer, carry):
            peer = far_pencil(n_peer)
            pltpu.make_async_remote_copy(
                src.at[(peer, *part)],
                dst.at[(p, *part)],
                send_sem.at[n],
                recv_sem.at[n],
                device_id={"pencil": peer},
                device_id_type=MESH,
            ).start()
            return carry

        lax.fori_loop(0, pencils - 1, one, 0)

    def all_but_one(ref, part, sem):
        view = ref.at[(pl.ds(0, pencils - 1), *part)]
        pltpu.make_async_copy(view, view, sem).wait()

    def wait_bytes(ref, i, count, sem):
        view = ref.at[i, pl.ds(0, count)]
        pltpu.make_async_copy(view, view, sem.at[i]).wait()

    images_direct(t, coils - 1)
    weight_copy.wait()
    frame_rows(other)
    images_direct(other, coils)
    for i in range(1, planes):
        images_to(i, t)
        images_to(i, other)
    images[:, me] = own_frames[t]
    bases[me] = own_base[...]
    for copy in loads[:3]:
        copy.wait()
    for i in range(planes):
        wait_bytes(images, i, owners - (1 if i == 0 else 5), irecv_sem)
        forward(i)
        if i == 0:
            for later in range(1, planes):
                relay(later)
    base_copy(me, base_cross, {"frame": other})

    for copy in loads[3:6]:
        copy.wait()
    all_but_one(recv_f, parts[0], frecv_sem.at[0])
    bases_along(me)
    partner = c * frames + other
    crossed = bases.at[partner]
    pltpu.make_async_copy(crossed, crossed, base_cross).wait()
    bases_along(partner)
    lines = jnp.concatenate(
        [recv_f[:, h, 0].reshape(-1, width) for h in range(halves)], axis=1
    )
    kspace[...] = dot(forward_z[0], lines) - kdata[...].astype(F32).reshape(kspace.shape)
    loads[6].wait()
    half_rows = kspace.shape[0] // 2
    for h in range(halves):
        columns = slice(h * width, (h + 1) * width)
        for i in range(1, planes):
            all_but_one(recv_f, (h, i), frecv_sem.at[1 + slabs.index((h, i))])
            lines = recv_f[:, h, i].reshape(-1, width)
            if i < planes - 1:
                kspace[:, columns] = dot(forward_z[i], lines) + kspace[:, columns]
        keep = sampling[:, columns].astype(F32)[:, None, :]
        for part in range(2):
            rows = slice(part * half_rows, (part + 1) * half_rows)
            value = dot(forward_z[planes - 1, rows, :], lines) + kspace[rows, columns]
            value = keep * value.reshape(keep.shape[0], -1, width)
            high, low = split(value.reshape(half_rows, width))
            residual[h, rows, :width] = high
            residual[h, rows, width:] = low
        for i in range(planes):
            x = dot(inverse_z[i], residual[h])
            x = (x[:, :width] + x[:, width:]).astype(BF16)
            send_b[:, h, i] = x.reshape(pencils, -1, width)
            recv_b[p, h, i] = send_b[p, h, i]
            exchange(send_b, recv_b, bsend_sem, brecv_sem, h * planes + i, (h, i))

    loads[7].wait()
    base_blocks = bases.at[pl.ds(0, owners - 1)]
    along_blocks = bases.at[pl.ds(0, owners - frames)]
    pltpu.make_async_copy(along_blocks, along_blocks, base_recv).wait()
    for i in range(planes):
        for h in range(halves):
            all_but_one(recv_b, (h, i), brecv_sem.at[h * planes + i])
        lines = jnp.concatenate(
            [recv_b[:, h, i].reshape(-1, width) for h in range(halves)], axis=1
        )
        x = dot(inverse_x[...], lines)
        high, low = split(x)
        y = dot(high, rows_y[...]) + dot(low, rows_y[...])
        back_re = y[:nx, :ny] - y[nx:, ny:]
        back_im = y[nx:, :ny] + y[:nx, ny:]
        sens_re = sens[0, i].astype(F32)
        sens_im = sens[1, i].astype(F32)
        adj_re = sens_re * back_re + sens_im * back_im
        adj_im = sens_re * back_im - sens_im * back_re
        base_re = bases[:, i, 0].reshape(nx, ny).astype(F32)
        base_im = bases[:, i, 1].reshape(nx, ny).astype(F32)
        terms = base_re * adj_re + base_im * adj_im
        send_p[i] = terms.astype(BF16).reshape(send_p.shape[1:])
        recv_p[i, me] = send_p[i, me]

        def hand(n, carry):
            coil, frame = far_owner(n)
            pltpu.make_async_remote_copy(
                send_p.at[i, coil * frames + frame],
                recv_p.at[i, me],
                psend_sem.at[i],
                precv_sem.at[i],
                device_id={"coil": coil, "frame": frame},
                device_id_type=MESH,
            ).start()
            return carry

        lax.fori_loop(0, owners - 1, hand, 0)

    for i in range(planes):
        wait_bytes(recv_p, i, owners - 1, precv_sem)
        for f in range(frames):
            total = sum(recv_p[i, n * frames + f].astype(F32) for n in range(coils))
            for n in range(2):
                out[n, f, i] = weights[f, n] * total

    for i in range(planes):
        wait_bytes(images, i, owners - 1, isend_sem)
        for h in range(halves):
            all_but_one(send_b, (h, i), bsend_sem.at[h * planes + i])
        wait_bytes(send_p, i, owners - 1, psend_sem)
    for n, part in enumerate(parts):
        all_but_one(send_f, part, fsend_sem.at[n])
    pltpu.make_async_copy(base_blocks, base_blocks, base_send).wait()


def solution(mesh):
    coils, pencils, frames = mesh.shape["coil"], mesh.shape["pencil"], mesh.shape["frame"]

    def per_device(
        kdata, sampling, sensitivity, baseline, ktrans, plasma_volume, arterial, arterial_integral
    ):
        planes, rows, ny = ktrans.shape
        nx = sensitivity.shape[3]
        nz = kdata.shape[3]
        lines = kdata.shape[4]
        owners = coils * frames
        tabs = all_tables(nx, ny, nz, pencils)
        hbm = pl.BlockSpec(memory_space=pltpu.HBM)
        smem = pl.BlockSpec(memory_space=pltpu.SMEM)
        vmem = pl.BlockSpec(memory_space=pltpu.VMEM)
        dma = pltpu.SemaphoreType.DMA
        halves = 2 if ny % 256 == 0 else 1
        blocks = (pencils, halves, planes, 2 * lines, ny // halves)
        out = pl.pallas_call(
            lambda *refs: kernel((coils, pencils, frames), *refs),
            out_shape=jax.ShapeDtypeStruct((2, frames, planes, rows, ny), F32),
            in_specs=[hbm, hbm, hbm, smem, smem] + [hbm] * 8,
            out_specs=vmem,
            scratch_shapes=[
                pltpu.VMEM((planes, 2, rows, ny), BF16),
                pltpu.VMEM((2, planes, rows, ny), BF16),
                pltpu.VMEM((frames, planes, 2, rows, ny), BF16),
                pltpu.VMEM((planes, owners, 2, rows, ny), BF16),
                pltpu.VMEM((owners, planes, 2, rows, ny), BF16),
                pltpu.VMEM((2, planes, nx, ny), BF16),
                pltpu.VMEM((2, nz, lines, ny), BF16),
                pltpu.VMEM((nz, ny), jnp.int32),
                *[pltpu.VMEM(tab.shape, BF16) for tab in tabs],
                pltpu.VMEM(blocks, BF16),
                pltpu.VMEM(blocks, BF16),
                pltpu.VMEM((2 * nz * lines, ny), F32),
                pltpu.VMEM((halves, 2 * nz * lines, 2 * ny // halves), BF16),
                pltpu.VMEM(blocks, BF16),
                pltpu.VMEM(blocks, BF16),
                pltpu.VMEM((planes, owners, rows, ny), BF16),
                pltpu.VMEM((planes, owners, rows, ny), BF16),
                pltpu.VMEM((frames, 2, rows, ny), F32),
                dma((4,)),
                dma((8,)),
                dma((planes,)),
                dma((planes,)),
                dma((planes, frames, 2)),
                dma,
                dma,
                dma,
                dma((1 + halves * (planes - 1),)),
                dma((1 + halves * (planes - 1),)),
                dma((planes * halves,)),
                dma((planes * halves,)),
                dma((planes,)),
                dma((planes,)),
                dma,
                dma,
            ],
            compiler_params=pltpu.CompilerParams(
                collective_id=0, has_side_effects=True, vmem_limit_bytes=56 * 1024 * 1024
            ),
        )(
            baseline,
            ktrans,
            plasma_volume,
            arterial,
            arterial_integral,
            sensitivity[0],
            kdata[0, 0],
            sampling[0],
            *[jnp.asarray(tab) for tab in tabs],
        )
        return tuple(sum(out[n, f] for f in range(frames)) for n in range(2))

    in_specs = (
        P("frame", "coil", None, None, "pencil", None),
        P("frame", None, None),
        P("coil", None, "pencil", None, None),
        P(None, "pencil", ("coil", "frame"), None),
        P("pencil", ("coil", "frame"), None),
        P("pencil", ("coil", "frame"), None),
        P("frame"),
        P("frame"),
    )
    out_specs = (P("pencil", ("coil", "frame"), None), P("pencil", ("coil", "frame"), None))
    return jax.shard_map(
        per_device, mesh=mesh, in_specs=in_specs, out_specs=out_specs, check_vma=False
    )
```
